32 devices in a mesh: grp: 16 (over z, y, x), cores: 2 (over core).
Axes of the slice: x: 2, y: 2, z: 4, core: 2. Of those that a mesh axis runs over, the one named last changes fastest.
Arguments:
- invariant_fluid_quantities: float32 [8, 2048, 512], P(None, ('grp', 'cores')), may hold values from -6 to 6
- flux_derivative_matrices: float32 [3, 8, 8], replicated, may hold values from -2 to 2
- levels: int32 [2048], P(('grp', 'cores')), may hold values from 0 to 3
- neighbours: int32 [2048, 6], P(('grp', 'cores')), may hold values from -1 to 2047, as said below
- block_latitude_band: int32 [2048, 1], P(('grp', 'cores')), may hold values from 0 to 15; in each aligned block of 64 rows (0 to 63, 64 to 127, ...) at most 8 rows name the same one
- block_longitude_segment: int32 [2048], P(('grp', 'cores')), may hold values from 0 to 15
- parallel_flow_coefficients: float32 [8], replicated, may hold values from -2 to 2
Outputs:
- state_out: float32 [8, 2048, 512], P(None, ('grp', 'cores'))
- fac_grid: float32 [64, 1024], P(('grp', 'cores'))
- potential: float32 [64, 1024], P(('grp', 'cores'))
- shell_potential: float32 [2048, 128], P(('grp', 'cores'))
The draws below stay inside these ranges and needn't reach their ends.
Inputs may be any that keep to these rules, and one draw needn't show every extreme that they name: `neighbours`: each entry is -1 or a block held by the same device as the block or by the device just before or after it; device i holds blocks i * 64 to (i + 1) * 64 - 1. `block_latitude_band`: among the 64 blocks of one device no band is named more than 8 times, a bound that some block reaches.
All inputs are finite; a program needn't handle non-finite values.
Results may differ from the reference program's by a relative error of at most 0.0004.
Values sent between devices are 32-bit elements; how exact they have to be, the bound alone decides.
A program may use at most 128 MiB of HBM per device.

```python
import math
import jax
import jax.numpy as jnp
import numpy as np
from jax import lax

FLUID_QUANTITIES = 8
CUBES_PER_CHIP = 64
LEVELS = 4
STEPS = 2
LAT_DEV = 2
NLON = 1024
DEGREES = 512
CUBE_COUNT = 2048
CAP = 8
NLAT = 64
SEGS = 16
N_GRP = 16
N_CORES = 2


def draw_neighbours(key, part):
    total = CUBES_PER_CHIP * N_GRP * N_CORES
    block_ids = jnp.arange(total, dtype=jnp.int32)
    owner = block_ids // CUBES_PER_CHIP
    offsets = jax.random.randint(key, (total, 6), -CUBES_PER_CHIP, 2 * CUBES_PER_CHIP, dtype=jnp.int32)
    candidate = owner[:, None] * CUBES_PER_CHIP + offsets
    result = jnp.where((candidate >= 0) & (candidate < total), candidate, -1)
    result = result.at[0, 0].set(-1)
    result = result.at[total - 2, 1].set(total - 1)
    return result.astype(jnp.int32)


def with_ends(array, own_key, low, top_value):
    shape = array.shape
    index_at = [jax.random.randint(jax.random.fold_in(own_key, axis), (), 0, shape[axis]) for axis in range(len(shape))]
    array = array.at[tuple(index_at)].set(low)
    longest = shape.index(max(shape))
    index_at[longest] = (index_at[longest] + 1) % shape[longest]
    return array.at[tuple(index_at)].set(top_value)


def block_scale(stream_key, dims, shards, smallest, high):
    def one(axis_at, shards_of):
        heights = jax.random.uniform(jax.random.fold_in(jax.random.fold_in(stream_key, 6), axis_at), (shards_of,), jnp.float32, smallest / len(shards), high / len(shards))
        return jnp.repeat(jnp.exp(heights), dims[axis_at] // shards_of).reshape((-1,) + (1,) * (len(dims) - axis_at - 1))

    level = one(*shards[0])
    for cut in shards[1:]:
        level = level * one(*cut)
    return level


def assign_block(rng, own, number, rows, count, top, bound, lean):
    sequence = jax.random.permutation(rng, count)
    crowded, common = shares(count, rows * top, bound, lean, True), shares(count, rows * top, bound, lean, False)
    places = jnp.arange(count)

    def named(tallies, turn):
        used = int((tallies > 0).sum())
        fixed = max(1, used // 4)
        moved = fixed + (places - fixed + turn * (used - fixed)) % max(1, count - fixed)
        return jnp.zeros((count,), jnp.int32).at[sequence[jnp.where(places < fixed, places, moved)]].set(jnp.asarray(tallies, jnp.int32))

    tallies = jnp.where(number % 4 == 0, named(crowded, number // 4), named(common, number - number // 4 - 1))
    mixed = jax.random.permutation(jax.random.fold_in(own, 3), count)
    giver, receiver = mixed[0:count // 2 * 2:2], mixed[1:count // 2 * 2:2]
    slack = jnp.minimum(tallies[giver] - 1, bound - tallies[receiver]) // 2
    slack = jnp.where((giver == sequence[0]) | (receiver == sequence[0]) | (tallies[receiver] == 0), 0, jnp.maximum(slack, 0))
    moved = jax.random.randint(jax.random.fold_in(own, 4), (count // 2,), 0, 1 << 20) % (slack + 1)
    tallies = tallies.at[giver].add(-moved).at[receiver].add(moved)
    items = jnp.searchsorted(jnp.cumsum(tallies), jnp.arange(rows * top), side="right").astype(jnp.int32)
    listing = items.reshape(top, rows).T
    listing = listing[jax.random.permutation(jax.random.fold_in(own, 1), rows)]
    turn = jax.random.randint(jax.random.fold_in(own, 2), (rows, 1), 0, top)
    return jnp.take_along_axis(listing, (jnp.arange(top)[None, :] + turn) % top, axis=1)


def shares(count, total, most, slope, full):
    portions = [(1 << 20) // math.isqrt(grade ** slope) + 1 for grade in range(1, count + 1)]
    largest = most if full else min(most, max(-(-total // count), total * portions[0] // sum(portions)))
    least = 1 if total - largest >= count - 1 else 0
    holding, surplus = [largest] + [least] * (count - 1), total - largest - least * (count - 1)
    while surplus > 0:
        candidates = [i for i in range(1, count) if holding[i] < largest] or [i for i in range(1, count) if holding[i] < most]
        whole, left = sum([portions[i] for i in candidates]), surplus
        for i in candidates:
            addition = min(most - holding[i], max(1, left * portions[i] // whole), surplus)
            holding[i] = holding[i] + addition
            surplus = surplus - addition
    return np.array(holding)


def normal_values(own_key, extent, spread, most, pieces=(), held_as=jnp.bfloat16):
    level = block_scale(own_key, extent, pieces, -0.22, 0.18) if pieces else 1.0
    array = jax.random.normal(own_key, extent, jnp.float32) * spread * level
    return jnp.minimum(jnp.maximum(array, -most), most).astype(held_as)


def setup_inputs(seed: int = 0) -> dict:
    key_list = jax.random.split(jax.random.key(seed), 8)
    invariant_fluid_quantities = normal_values(key_list[0], (FLUID_QUANTITIES, CUBE_COUNT, 512), 1.0, 6.0, ((1, 32),), jnp.float32)
    flux_derivative_matrices = normal_values(key_list[1], (3, FLUID_QUANTITIES, FLUID_QUANTITIES), FLUID_QUANTITIES ** -0.5, 2.0, (), jnp.float32)
    levels = with_ends(jax.random.randint(key_list[2], (CUBE_COUNT,), 0, LEVELS), jax.random.fold_in(key_list[2], 1), 0, LEVELS - 1).astype(jnp.int32)
    neighbours = draw_neighbours(jax.random.fold_in(key_list[7], 71), 0)
    block_latitude_band_keys = jax.random.split(jax.random.fold_in(key_list[4], 1), CUBE_COUNT // CUBES_PER_CHIP)
    block_latitude_band_turns = jax.random.permutation(jax.random.fold_in(key_list[4], 3), CUBE_COUNT // CUBES_PER_CHIP)
    block_latitude_band = jax.vmap(lambda own, number: assign_block(jax.random.fold_in(key_list[4], 2), own, number, CUBES_PER_CHIP, N_GRP, 1, CAP, 2))(block_latitude_band_keys, block_latitude_band_turns).reshape((CUBE_COUNT, 1))
    block_longitude_segment = with_ends(jax.random.randint(key_list[5], (CUBE_COUNT,), 0, SEGS), jax.random.fold_in(key_list[5], 1), 0, SEGS - 1).astype(jnp.int32)
    parallel_flow_coefficients = normal_values(key_list[6], (FLUID_QUANTITIES,), FLUID_QUANTITIES ** -0.5, 2.0, (), jnp.float32)
    return {"invariant_fluid_quantities": invariant_fluid_quantities, "flux_derivative_matrices": flux_derivative_matrices, "levels": levels, "neighbours": neighbours, "block_latitude_band": block_latitude_band, "block_longitude_segment": block_longitude_segment, "parallel_flow_coefficients": parallel_flow_coefficients}


COURANT = 0.3
KAPPA2 = 400.0
POT_GAIN = 2000.0
HIGHEST_PRECISION = lax.Precision.HIGHEST

def block_faces(state_in):
    state_variables, blocks = (state_in.shape[0], state_in.shape[1])
    block_cube = state_in.reshape(state_variables, blocks, 8, 8, 8)
    layers = [block_cube[:, :, 0], block_cube[:, :, 7], block_cube[:, :, :, 0], block_cube[:, :, :, 7], block_cube[:, :, :, :, 0], block_cube[:, :, :, :, 7]]
    return jnp.stack([one_layer.reshape(state_variables, blocks, 64) for one_layer in layers], axis=2)

def spread_face(values, direction):
    state_variables, blocks = (values.shape[0], values.shape[1])
    if direction == 0:
        expanded = jnp.broadcast_to(values.reshape(state_variables, blocks, 1, 64), (state_variables, blocks, 8, 64))
    elif direction == 1:
        expanded = jnp.broadcast_to(values.reshape(state_variables, blocks, 8, 1, 8), (state_variables, blocks, 8, 8, 8))
    else:
        expanded = jnp.broadcast_to(values.reshape(state_variables, blocks, 64, 1), (state_variables, blocks, 64, 8))
    return expanded.reshape(state_variables, blocks, 512)

def ghost_values(own_faces, face_table, index):
    result = []
    for face_index in range(6):
        column = index[:, face_index]
        fetched = jnp.take(face_table[:, :, face_index ^ 1], jnp.maximum(column, 0), axis=1)
        selected = jnp.where(column[None, :, None] >= 0, fetched, own_faces[:, :, face_index])
        result.append(spread_face(selected, face_index // 2))
    return result

def wave_speeds(flux_derivative_matrices):
    return lax.optimization_barrier(jnp.max(lax.optimization_barrier(jnp.sum(jnp.abs(flux_derivative_matrices), axis=2)), axis=1))

def advance(state_in, flux_derivative_matrices, speeds, rate_block, ghosts):
    position = jnp.arange(512, dtype=jnp.int32)
    change = jnp.zeros(state_in.shape, jnp.float32)
    for direction in range(3):
        stride = 64 // 8 ** direction
        coordinate = position // stride % 8
        lower_side = jnp.where(coordinate == 0, ghosts[2 * direction], jnp.roll(state_in, stride, axis=2))
        upper_side = jnp.where(coordinate == 7, ghosts[2 * direction + 1], jnp.roll(state_in, -stride, axis=2))
        difference = jnp.einsum('ij,jbp->ibp', flux_derivative_matrices[direction], upper_side - lower_side, precision=HIGHEST_PRECISION)
        change = change + 0.5 * difference - 0.5 * speeds[direction] * (upper_side - 2.0 * state_in + lower_side)
    return state_in - rate_block[None, :, None] * change

def shell_currents(state_in, parallel_flow_coefficients):
    state_variables, blocks = (state_in.shape[0], state_in.shape[1])
    inner_cells = state_in.reshape(state_variables, blocks, 64, 8)[:, :, :, 0:2]
    inner_cells = jnp.swapaxes(inner_cells, 2, 3).reshape(state_variables, blocks, 128)
    return jnp.einsum('v,vbk->bk', parallel_flow_coefficients, inner_cells, precision=HIGHEST_PRECISION)

def fourier_tables(orders):
    longitudes = jnp.arange(NLON, dtype=jnp.int32)
    phase_index = longitudes[:, None] * orders[None, :] % NLON
    angle_rad = phase_index.astype(jnp.float32) * (2.0 * math.pi / NLON)
    return (jnp.cos(angle_rad), jnp.sin(angle_rad))

def legendre_start(sine_lat, orders):
    series_k = jnp.arange(1, DEGREES, dtype=jnp.int32).astype(jnp.float32)
    log_sums = jnp.concatenate([jnp.zeros((1,), jnp.float32), jnp.cumsum(0.5 * jnp.log((2.0 * series_k + 1.0) / (2.0 * series_k)))])
    log_base = jnp.take(log_sums, orders)
    order_real = orders.astype(jnp.float32)
    return jnp.exp(0.5 * math.log(0.5) + log_base[None, :] + order_real[None, :] * jnp.log(sine_lat)[:, None])

def legendre_next(degree, orders, cosine_lat, diagonal, previous, before):
    degree_real = degree.astype(jnp.float32)
    order_real = orders.astype(jnp.float32)[None, :]
    order_int = orders[None, :]
    cosine_col = cosine_lat[:, None]
    ratio_up = jnp.sqrt(jnp.maximum(4.0 * degree_real * degree_real - 1.0, 1.0) / jnp.maximum(degree_real * degree_real - order_real * order_real, 1.0))
    lower_deg = degree_real - 1.0
    ratio_back = jnp.sqrt(jnp.maximum(lower_deg * lower_deg - order_real * order_real, 0.0) / jnp.maximum(4.0 * lower_deg * lower_deg - 1.0, 1.0))
    coef_prev = jnp.where(degree == order_int + 1, jnp.sqrt(2.0 * order_real + 3.0) * cosine_col, jnp.where(degree >= order_int + 2, ratio_up * cosine_col, 0.0))
    coef_before = jnp.where(degree >= order_int + 2, -ratio_up * ratio_back, 0.0)
    injected = jnp.where(degree == order_int, diagonal, 0.0)
    return coef_prev * previous + coef_before * before + injected

def solve_spectral(coef_re, coef_im, cosine_lat, sine_lat, weights_lat, orders):
    diagonal = legendre_start(sine_lat, orders)
    zero_state = jnp.zeros(diagonal.shape, jnp.float32)

    def one_degree(carried, degree):
        previous, before, acc_re, acc_im = carried
        present = legendre_next(degree, orders, cosine_lat, diagonal, previous, before)
        weighted = weights_lat[:, None] * present
        spec_re = lax.optimization_barrier(jnp.sum(coef_re * weighted, axis=0))
        spec_im = lax.optimization_barrier(jnp.sum(coef_im * weighted, axis=0))
        degree_real = degree.astype(jnp.float32)
        gain_deg = POT_GAIN / (degree_real * (degree_real + 1.0) + KAPPA2)
        acc_re = acc_re + (gain_deg * spec_re)[None, :] * present
        acc_im = acc_im + (gain_deg * spec_im)[None, :] * present
        return ((present, previous, acc_re, acc_im), None)
    carried, _ = lax.scan(one_degree, (zero_state, zero_state, zero_state, zero_state), jnp.arange(DEGREES, dtype=jnp.int32))
    return (carried[2], carried[3])

def reference(invariant_fluid_quantities, flux_derivative_matrices, levels, neighbours, block_latitude_band, block_longitude_segment, parallel_flow_coefficients):
    speeds = wave_speeds(flux_derivative_matrices)
    rate_block = COURANT * jnp.exp2(levels.astype(jnp.float32) - (LEVELS - 1)) / jnp.max(speeds)
    batches_list = CUBE_COUNT // CUBES_PER_CHIP
    parallel_flow_charge = invariant_fluid_quantities
    for section_index in range(STEPS):
        face_table = block_faces(parallel_flow_charge)

        def step_group(inputs):
            group_state, group_index, group_rate = inputs
            own_faces = block_faces(group_state)
            ghosts = ghost_values(own_faces, face_table, group_index)
            return advance(group_state, flux_derivative_matrices, speeds, group_rate, ghosts)
        batched_together = jnp.moveaxis(parallel_flow_charge.reshape(FLUID_QUANTITIES, batches_list, CUBES_PER_CHIP, 512), 1, 0)
        advanced_forward = lax.map(step_group, (batched_together, neighbours.reshape(batches_list, CUBES_PER_CHIP, 6), rate_block.reshape(batches_list, CUBES_PER_CHIP)))
        parallel_flow_charge = jnp.moveaxis(advanced_forward, 0, 1).reshape(FLUID_QUANTITIES, CUBE_COUNT, 512)
    patches = shell_currents(parallel_flow_charge, parallel_flow_coefficients)
    block_ids = jnp.arange(CUBE_COUNT, dtype=jnp.int32)
    core_of = block_ids // CUBES_PER_CHIP % N_CORES
    first_lat = LAT_DEV * (N_CORES * block_latitude_band[:, 0] + core_of)
    cell_k = jnp.arange(128, dtype=jnp.int32)
    lat_rows = first_lat[:, None] + cell_k[None, :] // 64
    lon_cols = block_longitude_segment[:, None] * 64 + cell_k[None, :] % 64
    flat_cells = (lat_rows * NLON + lon_cols).astype(jnp.int32)
    fac_grid = jax.ops.segment_sum(patches.reshape(-1), flat_cells.reshape(-1), num_segments=NLAT * NLON).reshape(NLAT, NLON)
    orders = jnp.arange(DEGREES, dtype=jnp.int32)
    cos_table, sin_table = fourier_tables(orders)
    coef_re = jnp.dot(fac_grid, cos_table, precision=HIGHEST_PRECISION) / NLON
    coef_im = -jnp.dot(fac_grid, sin_table, precision=HIGHEST_PRECISION) / NLON
    lat_ids = jnp.arange(NLAT, dtype=jnp.int32)
    colatitude = (lat_ids.astype(jnp.float32) + 0.5) * (math.pi / NLAT)
    cosine_lat = jnp.cos(colatitude)
    sine_lat = jnp.sin(colatitude)
    weights_lat = math.pi / NLAT * sine_lat
    synth_re, synth_im = solve_spectral(coef_re, coef_im, cosine_lat, sine_lat, weights_lat, orders)
    factor = jnp.where(orders == 0, jnp.float32(1.0), jnp.float32(2.0))
    potential = jnp.dot(synth_re * factor, cos_table.T, precision=HIGHEST_PRECISION) - jnp.dot(synth_im * factor, sin_table.T, precision=HIGHEST_PRECISION)
    shell_potential = jnp.take(potential.reshape(-1), flat_cells)
    return (parallel_flow_charge, fac_grid, potential, shell_potential)
```

```python
import functools
import math

import jax
import jax.numpy as jnp
from jax import lax
from jax.experimental import pallas as pl
from jax.experimental.pallas import tpu as pltpu
from jax.sharding import PartitionSpec as P

LEVELS = 4
STEPS = 2
LAT_DEV = 2
NLON = 1024
DEGREES = 512


COURANT = 0.3
KAPPA2 = 400.0
POT_GAIN = 2000.0
HIGHEST_PRECISION = lax.Precision.HIGHEST


def passed_along(value, axis, steps):
    count = lax.axis_size(axis)
    leading, last = (max(0, -steps), min(count, count - steps))
    return lax.ppermute(value, axis, [(source, source + steps) for source in range(leading, last)])


def block_faces(state_in):
    state_variables, blocks = (state_in.shape[0], state_in.shape[1])
    block_cube = state_in.reshape(state_variables, blocks, 8, 8, 8)
    layers = [
        block_cube[:, :, 0],
        block_cube[:, :, 7],
        block_cube[:, :, :, 0],
        block_cube[:, :, :, 7],
        block_cube[:, :, :, :, 0],
        block_cube[:, :, :, :, 7],
    ]
    return jnp.stack(
        [one_layer.reshape(state_variables, blocks, 64) for one_layer in layers], axis=2
    )


def spread_face(values, direction):
    state_variables, blocks = (values.shape[0], values.shape[1])
    if direction == 0:
        expanded = jnp.broadcast_to(
            values.reshape(state_variables, blocks, 1, 64), (state_variables, blocks, 8, 64)
        )
    elif direction == 1:
        expanded = jnp.broadcast_to(
            values.reshape(state_variables, blocks, 8, 1, 8), (state_variables, blocks, 8, 8, 8)
        )
    else:
        expanded = jnp.broadcast_to(
            values.reshape(state_variables, blocks, 64, 1), (state_variables, blocks, 64, 8)
        )
    return expanded.reshape(state_variables, blocks, 512)


def ghost_values(own_faces, face_table, index):
    result = []
    for face_index in range(6):
        column = index[:, face_index]
        fetched = jnp.take(face_table[:, :, face_index ^ 1], jnp.maximum(column, 0), axis=1)
        selected = jnp.where(column[None, :, None] >= 0, fetched, own_faces[:, :, face_index])
        result.append(spread_face(selected, face_index // 2))
    return result


def wave_speeds(flux_derivative_matrices):
    return jnp.max(jnp.sum(jnp.abs(flux_derivative_matrices), axis=2), axis=1)


def advance(state_in, flux_derivative_matrices, speeds, rate_block, ghosts):
    position = jnp.arange(512, dtype=jnp.int32)
    change = jnp.zeros(state_in.shape, jnp.float32)
    for direction in range(3):
        stride = 64 // 8**direction
        coordinate = position // stride % 8
        lower_side = jnp.where(
            coordinate == 0, ghosts[2 * direction], jnp.roll(state_in, stride, axis=2)
        )
        upper_side = jnp.where(
            coordinate == 7, ghosts[2 * direction + 1], jnp.roll(state_in, -stride, axis=2)
        )
        difference = jnp.einsum(
            "ij,jbp->ibp",
            flux_derivative_matrices[direction],
            upper_side - lower_side,
            precision=HIGHEST_PRECISION,
        )
        change = (
            change
            + 0.5 * difference
            - 0.5 * speeds[direction] * (upper_side - 2.0 * state_in + lower_side)
        )
    return state_in - rate_block[None, :, None] * change


def shell_currents(state_in, parallel_flow_coefficients):
    state_variables, blocks = (state_in.shape[0], state_in.shape[1])
    inner_cells = state_in.reshape(state_variables, blocks, 64, 8)[:, :, :, 0:2]
    inner_cells = jnp.swapaxes(inner_cells, 2, 3).reshape(state_variables, blocks, 128)
    return jnp.einsum(
        "v,vbk->bk", parallel_flow_coefficients, inner_cells, precision=HIGHEST_PRECISION
    )


def fourier_tables(orders):
    longitudes = jnp.arange(NLON, dtype=jnp.int32)
    phase_index = longitudes[:, None] * orders[None, :] % NLON
    angle_rad = phase_index.astype(jnp.float32) * (2.0 * math.pi / NLON)
    return (jnp.cos(angle_rad), jnp.sin(angle_rad))


def legendre_start(sine_lat, orders):
    series_k = jnp.arange(1, DEGREES, dtype=jnp.int32).astype(jnp.float32)
    log_sums = jnp.concatenate(
        [
            jnp.zeros((1,), jnp.float32),
            jnp.cumsum(0.5 * jnp.log((2.0 * series_k + 1.0) / (2.0 * series_k))),
        ]
    )
    log_base = jnp.take(log_sums, orders)
    order_real = orders.astype(jnp.float32)
    return jnp.exp(
        0.5 * math.log(0.5) + log_base[None, :] + order_real[None, :] * jnp.log(sine_lat)[:, None]
    )


def pair_kernel(share_rows, start_ref, order_ref, cosine_ref, weight_ref, out_ref, table):
    diagonal = start_ref[...]
    height, pieces = diagonal.shape[0], diagonal.shape[1] // 128
    order = order_ref[...]
    square = order * order
    cosine = cosine_ref[...]

    def one_degree(degree, carried):
        previous, before = carried
        real = degree.astype(jnp.float32)
        top = jnp.full(diagonal.shape, 4.0 * real * real - 1.0, jnp.float32)
        lower = real - 1.0
        low = jnp.full(diagonal.shape, 4.0 * lower * lower - 1.0, jnp.float32)
        up = jnp.sqrt(jnp.maximum(top, 1.0) / jnp.maximum(real * real - square, 1.0))
        back = jnp.sqrt(jnp.maximum(lower * lower - square, 0.0) / jnp.maximum(low, 1.0))
        present = (up * cosine) * previous + (-up * back) * before
        present = present + jnp.where(order == real, diagonal, 0.0)
        at = pl.multiple_of(degree * height, height)
        for piece in range(pieces):
            table[piece, pl.ds(at, height), :] = present[:, 128 * piece : 128 * (piece + 1)]
        return present, previous

    zero = diagonal * 0.0
    lax.fori_loop(0, DEGREES, one_degree, (zero, zero), unroll=8)
    degrees = lax.broadcasted_iota(jnp.int32, (DEGREES, 1), 0).astype(jnp.float32)
    gain = POT_GAIN / (degrees * (degrees + 1.0) + KAPPA2)
    for row in range(share_rows):
        rows = jnp.concatenate(
            [table[piece, pl.ds(row, DEGREES, stride=height), :] for piece in range(pieces)], axis=1
        )
        out_ref[row] = lax.dot_general(
            rows * weight_ref[...],
            rows * gain,
            (((0,), (0,)), ((), ())),
            precision=HIGHEST_PRECISION,
            preferred_element_type=jnp.float32,
        )


def order_pairs(sine_lat, cosine_lat, weights_lat, orders):
    lat_total, share = sine_lat.shape[0], orders.shape[0]
    side = max(1, min(share, 128 // lat_total))
    share_rows, lanes = share // side, side * lat_total
    start = legendre_start(sine_lat, orders).T.reshape(side, share_rows, lat_total)
    start = jnp.swapaxes(start, 0, 1).reshape(share_rows, lanes)
    order_real = jnp.broadcast_to(
        orders.astype(jnp.float32).reshape(side, share_rows, 1), (side, share_rows, lat_total)
    )
    order_real = jnp.swapaxes(order_real, 0, 1).reshape(share_rows, lanes)
    height = -(-share_rows // 8) * 8
    start = jnp.pad(start, ((0, height - share_rows), (0, 0)))
    order_real = jnp.pad(order_real, ((0, height - share_rows), (0, 0)))
    cosine = jnp.tile(cosine_lat, side)[None, :]
    weight = jnp.tile(weights_lat, side)[None, :]
    pairs = pl.pallas_call(
        functools.partial(pair_kernel, share_rows),
        out_shape=jax.ShapeDtypeStruct((share_rows, lanes, lanes), jnp.float32),
        scratch_shapes=[pltpu.VMEM((lanes // 128, DEGREES * height, 128), jnp.float32)],
        compiler_params=pltpu.CompilerParams(vmem_limit_bytes=48 * 1024 * 1024),
    )(start, order_real, cosine, weight)
    blocks = [
        pairs[:, lat_total * at : lat_total * (at + 1), lat_total * at : lat_total * (at + 1)]
        for at in range(side)
    ]
    return jnp.concatenate(blocks, axis=0)


def solve_spectral(coef_re, coef_im, cosine_lat, sine_lat, weights_lat, orders):
    pairs = order_pairs(sine_lat, cosine_lat, weights_lat, orders)
    both = jnp.stack([coef_re.T, coef_im.T], axis=1)
    synth = jnp.einsum("rcj,rjk->crk", both, pairs, precision=HIGHEST_PRECISION)
    return (synth[0].T, synth[1].T)


def body(
    invariant_fluid_quantities,
    flux_derivative_matrices,
    levels,
    neighbours,
    block_latitude_band,
    block_longitude_segment,
    parallel_flow_coefficients,
):
    grp_size = lax.axis_size("grp")
    core_size = lax.axis_size("cores")
    device_total = grp_size * core_size
    block_portion = invariant_fluid_quantities.shape[1]
    state_variables = invariant_fluid_quantities.shape[0]
    device = lax.axis_index(("grp", "cores"))
    speeds = wave_speeds(flux_derivative_matrices)
    rate_block = COURANT * jnp.exp2(levels.astype(jnp.float32) - (LEVELS - 1)) / jnp.max(speeds)
    offset = (device - 1) * block_portion
    local_index = jnp.where(neighbours >= 0, neighbours - offset, -1)
    parallel_flow_charge = invariant_fluid_quantities
    for section_index in range(STEPS):
        own_faces = block_faces(parallel_flow_charge)
        flat_faces = own_faces.reshape(state_variables, block_portion, 384)
        faces_prev = passed_along(flat_faces, ("grp", "cores"), 1)
        faces_next = passed_along(flat_faces, ("grp", "cores"), -1)
        face_table = jnp.concatenate([faces_prev, flat_faces, faces_next], axis=1).reshape(
            state_variables, 3 * block_portion, 6, 64
        )
        ghosts = ghost_values(own_faces, face_table, local_index)
        parallel_flow_charge = advance(
            parallel_flow_charge, flux_derivative_matrices, speeds, rate_block, ghosts
        )
    patches = shell_currents(parallel_flow_charge, parallel_flow_coefficients)
    band_index = block_latitude_band[:, 0]
    block_ids = jnp.arange(block_portion, dtype=jnp.int32)
    earlier = (band_index[None, :] == band_index[:, None]) & (
        block_ids[None, :] < block_ids[:, None]
    )
    rank_in_band = jnp.sum(earlier.astype(jnp.int32), axis=1)
    capacity = max(2, 2 * block_portion // grp_size)
    slot_index = band_index * capacity + rank_in_band
    slot_ids = jnp.arange(grp_size * capacity, dtype=jnp.int32)
    placing = (slot_ids[:, None] == slot_index[None, :]).astype(jnp.float32)
    send_rows = jnp.dot(placing, patches, precision=HIGHEST_PRECISION).reshape(
        grp_size, capacity, 128
    )
    send_codes = jnp.dot(
        placing, (block_longitude_segment + 1).astype(jnp.float32), precision=HIGHEST_PRECISION
    ).reshape(grp_size, capacity)
    got_rows, got_codes = (
        lax.all_to_all(send_rows, "grp", split_axis=0, concat_axis=0, tiled=True),
        lax.all_to_all(send_codes, "grp", split_axis=0, concat_axis=0, tiled=True),
    )
    segments = NLON // 64
    segment_codes = jnp.arange(1, segments + 1, dtype=jnp.int32).astype(jnp.float32)
    landing = (got_codes.reshape(-1)[:, None] == segment_codes[None, :]).astype(jnp.float32)
    gathered = jnp.dot(landing.T, got_rows.reshape(-1, 128), precision=HIGHEST_PRECISION)
    fac_local = jnp.swapaxes(gathered.reshape(segments, LAT_DEV, 64), 0, 1).reshape(LAT_DEV, NLON)
    orders_all = jnp.arange(DEGREES, dtype=jnp.int32)
    cos_table, sin_table = fourier_tables(orders_all)
    coef_re = jnp.dot(fac_local, cos_table, precision=HIGHEST_PRECISION) / NLON
    coef_im = -jnp.dot(fac_local, sin_table, precision=HIGHEST_PRECISION) / NLON
    lat_total = LAT_DEV * device_total
    degree_share = DEGREES // device_total
    lat_ids = jnp.arange(lat_total, dtype=jnp.int32)
    colatitude = (lat_ids.astype(jnp.float32) + 0.5) * (math.pi / lat_total)
    cosine_all = jnp.cos(colatitude)
    sine_all = jnp.sin(colatitude)
    weights_all = math.pi / lat_total * sine_all
    own_orders = device * degree_share + jnp.arange(degree_share, dtype=jnp.int32)
    stacked = jnp.stack([coef_re, coef_im])
    regrouped = lax.all_to_all(
        lax.all_to_all(stacked, "grp", split_axis=2, concat_axis=1, tiled=True),
        "cores",
        split_axis=2,
        concat_axis=1,
        tiled=True,
    )
    regrouped = jnp.transpose(
        regrouped.reshape(2, core_size, grp_size, LAT_DEV, degree_share), (0, 2, 1, 3, 4)
    ).reshape(2, lat_total, degree_share)
    synth_re, synth_im = solve_spectral(
        regrouped[0], regrouped[1], cosine_all, sine_all, weights_all, own_orders
    )
    synth_both = jnp.stack([synth_re, synth_im])
    returned = lax.all_to_all(
        lax.all_to_all(synth_both, "grp", split_axis=1, concat_axis=2, tiled=True),
        "cores",
        split_axis=1,
        concat_axis=2,
        tiled=True,
    )
    column_ids = jnp.arange(DEGREES, dtype=jnp.int32)
    order_perm = (
        degree_share
        * (
            core_size * (column_ids // degree_share % grp_size)
            + column_ids // (grp_size * degree_share)
        )
        + column_ids % degree_share
    )
    cos_perm, sin_perm = fourier_tables(order_perm)
    factor = jnp.where(order_perm == 0, jnp.float32(1.0), jnp.float32(2.0))
    potential_local = jnp.dot(
        returned[0] * factor, cos_perm.T, precision=HIGHEST_PRECISION
    ) - jnp.dot(returned[1] * factor, sin_perm.T, precision=HIGHEST_PRECISION)
    grid_segments = jnp.swapaxes(potential_local.reshape(LAT_DEV, segments, 64), 0, 1).reshape(
        segments, 128
    )
    back_rows = jnp.dot(landing, grid_segments, precision=HIGHEST_PRECISION).reshape(
        grp_size, capacity, 128
    )
    home_rows = lax.all_to_all(back_rows, "grp", split_axis=0, concat_axis=0, tiled=True)
    shell_potential = jnp.dot(placing.T, home_rows.reshape(-1, 128), precision=HIGHEST_PRECISION)
    return (parallel_flow_charge, fac_local, potential_local, shell_potential)


def solution(mesh):
    placed = (
        P(None, ("grp", "cores"), None),
        P(),
        P(("grp", "cores")),
        P(("grp", "cores"), None),
        P(("grp", "cores"), None),
        P(("grp", "cores")),
        P(),
    )
    return jax.shard_map(
        body,
        mesh=mesh,
        in_specs=placed,
        out_specs=(
            P(None, ("grp", "cores"), None),
            P(("grp", "cores"), None),
            P(("grp", "cores"), None),
            P(("grp", "cores"), None),
        ),
        check_vma=False,
    )
```

```python
import functools
import math

import jax
import jax.numpy as jnp
from jax import lax
from jax.experimental import pallas as pl
from jax.experimental.pallas import tpu as pltpu
from jax.sharding import PartitionSpec as P

LEVELS = 4
STEPS = 2
LAT_DEV = 2
NLON = 1024
DEGREES = 512


COURANT = 0.3
KAPPA2 = 400.0
POT_GAIN = 2000.0
HIGHEST_PRECISION = lax.Precision.HIGHEST


def wave_speeds(flux_derivative_matrices):
    return jnp.max(jnp.sum(jnp.abs(flux_derivative_matrices), axis=2), axis=1)


def split_dot(values, picks):
    high = values.astype(jnp.bfloat16)
    low = (values - high.astype(jnp.float32)).astype(jnp.bfloat16)
    return jnp.dot(high, picks, preferred_element_type=jnp.float32) + jnp.dot(
        low, picks, preferred_element_type=jnp.float32
    )


def halo_kernel(
    state_ref, flux_ref, speed_ref, coef_ref, rate_ref, target_ref,
    state_out, patch_out,
    cells, diffs, laps, change, own, before, after, picks,
    send_prev, send_next, recv_prev, recv_next,
):
    variables, blocks = state_ref.shape[0], state_ref.shape[1]
    lanes = 2 * blocks
    core_size = lax.axis_size("cores")
    total = lax.axis_size("grp") * core_size
    device = lax.axis_index("grp") * core_size + lax.axis_index("cores")
    has_prev, has_next = device > 0, device < total - 1
    prev_id = (lax.div(device - 1, core_size), lax.rem(device - 1 + core_size, core_size))
    next_id = (lax.div(device + 1, core_size), lax.rem(device + 1, core_size))
    mesh_type = pl.DeviceIdType.MESH
    barrier = pltpu.get_barrier_semaphore()

    @pl.when(has_prev)
    def _():
        pl.semaphore_signal(barrier, inc=1, device_id=prev_id, device_id_type=mesh_type)

    @pl.when(has_next)
    def _():
        pl.semaphore_signal(barrier, inc=1, device_id=next_id, device_id_type=mesh_type)

    @pl.when(jnp.logical_not(has_prev))
    def _():
        before[...] = jnp.zeros_like(before)

    @pl.when(jnp.logical_not(has_next))
    def _():
        after[...] = jnp.zeros_like(after)

    left_half = lax.broadcasted_iota(jnp.int32, (1, lanes), 1) < blocks
    for v in range(variables):
        both = jnp.concatenate([state_ref[v, :, 0:256], state_ref[v, :, 256:512]], axis=0)
        cells[v] = both.T

    def copies(step, direction):
        to_prev = pltpu.make_async_remote_copy(
            src_ref=own.at[step, direction], dst_ref=after.at[step, direction],
            send_sem=send_prev.at[step, direction], recv_sem=recv_next.at[step, direction],
            device_id=prev_id, device_id_type=mesh_type,
        )
        to_next = pltpu.make_async_remote_copy(
            src_ref=own.at[step, direction], dst_ref=before.at[step, direction],
            send_sem=send_next.at[step, direction], recv_sem=recv_prev.at[step, direction],
            device_id=next_id, device_id_type=mesh_type,
        )
        return to_prev, to_next

    def start(step, direction):
        to_prev, to_next = copies(step, direction)

        @pl.when(has_prev)
        def _():
            to_prev.start()

        @pl.when(has_next)
        def _():
            to_next.start()

    def arrive(step, direction):
        to_prev, to_next = copies(step, direction)

        @pl.when(has_prev)
        def _():
            to_next.wait_recv()

        @pl.when(has_next)
        def _():
            to_prev.wait_recv()

    def left(step, direction):
        to_prev, to_next = copies(step, direction)

        @pl.when(has_prev)
        def _():
            to_prev.wait_send()

        @pl.when(has_next)
        def _():
            to_next.wait_send()

    def fill(step, direction):
        for v in range(variables):
            if direction == 0:
                own[step, 0, pl.ds(64 * v, 64), :] = jnp.where(
                    left_half, cells[v, 0:64, :], cells[v, 192:256, :]
                )
            elif direction == 1:
                for side in range(2):
                    for x in range(4):
                        own[step, 1, pl.ds(256 * side + 32 * v + 8 * x, 8), :] = cells[
                            v, pl.ds(64 * x + 56 * side, 8), :
                        ]
            else:
                for side in range(2):
                    own[step, 2, pl.ds(256 * side + 32 * v, 32), :] = cells[
                        v, pl.ds(7 * side, 32, stride=8), :
                    ]

    def gathered(step, direction, first, rows, face):
        part = pl.ds(first, rows)
        table = jnp.concatenate(
            [before[step, direction, part, :], own[step, direction, part, :], after[step, direction, part, :]],
            axis=1,
        )
        return split_dot(table, picks[face])

    def keep(v, at, rows, lower, upper, here):
        diffs[v, pl.ds(at, rows), :] = upper - lower
        laps[v, pl.ds(at, rows), :] = upper - 2.0 * here + lower

    def sides(step, direction):
        if direction == 0:
            known = target_ref[0:1, :] >= 0
            ghosts = gathered(step, 0, 0, 64 * variables, 0)
            for v in range(variables):
                ghost = jnp.where(known, ghosts[64 * v : 64 * v + 64], own[step, 0, pl.ds(64 * v, 64), :])
                slabs = [cells[v, pl.ds(64 * x, 64), :] for x in range(4)]
                first = jnp.where(left_half, ghost, pltpu.roll(slabs[3], blocks, 1))
                last = jnp.where(left_half, pltpu.roll(slabs[0], blocks, 1), ghost)
                line = [first] + slabs + [last]
                for x in range(4):
                    keep(v, 64 * x, 64, line[x], line[x + 2], slabs[x])
            return
        near, far = 2 * direction - 1, 2 * direction
        rows = 32 * variables
        low = gathered(step, direction, rows, rows, near)
        high = gathered(step, direction, 0, rows, far)
        know_low, know_high = target_ref[near : near + 1, :] >= 0, target_ref[far : far + 1, :] >= 0
        for v in range(variables):
            part = slice(32 * v, 32 * v + 32)
            low_v = jnp.where(know_low, low[part], own[step, direction, pl.ds(32 * v, 32), :])
            high_v = jnp.where(know_high, high[part], own[step, direction, pl.ds(rows + 32 * v, 32), :])
            if direction == 1:
                for x in range(4):
                    slab = cells[v, pl.ds(64 * x, 64), :]
                    lower = jnp.concatenate([low_v[8 * x : 8 * x + 8], slab[0:56]], axis=0)
                    upper = jnp.concatenate([slab[8:64], high_v[8 * x : 8 * x + 8]], axis=0)
                    keep(v, 64 * x, 64, lower, upper, slab)
            else:
                whole = cells[v].reshape(32, 8, lanes)
                height = lax.broadcasted_iota(jnp.int32, (32, 8, lanes), 1)
                lower = jnp.where(height == 0, low_v[:, None, :], pltpu.roll(whole, 1, 1))
                upper = jnp.where(height == 7, high_v[:, None, :], pltpu.roll(whole, 7, 1))
                keep(v, 0, 256, lower.reshape(256, lanes), upper.reshape(256, lanes), cells[v])

    def mix(direction, final):
        rows = 16

        def one_chunk(chunk, carry):
            part = pl.ds(pl.multiple_of(chunk * rows, rows), rows)
            steps = [diffs[v, part, :] for v in range(variables)]
            for i in range(variables):
                total_i = -speed_ref[direction] * laps[i, part, :]
                for j in range(variables):
                    total_i = total_i + flux_ref[(direction * variables + i) * variables + j] * steps[j]
                if direction > 0:
                    total_i = total_i + change[i, part, :]
                if final:
                    cells[i, part, :] = cells[i, part, :] - rate_ref[0:1, :] * total_i
                else:
                    change[i, part, :] = total_i
            return carry

        lax.fori_loop(0, 256 // rows, one_chunk, 0)

    fill(0, 0)

    pl.semaphore_wait(barrier, has_prev.astype(jnp.int32) + has_next.astype(jnp.int32))
    for step in range(STEPS):
        for direction in range(3):
            if step > 0 or direction > 0:
                fill(step, direction)
            start(step, direction)
        if step == 0:
            row_ids = lax.broadcasted_iota(jnp.int32, (3 * lanes, lanes), 0)
            for face in range(5):
                hit = row_ids == target_ref[face : face + 1, :]
                picks[face] = hit.astype(jnp.float32).astype(jnp.bfloat16)
        for direction in range(3):
            arrive(step, direction)
            sides(step, direction)
            mix(direction, direction == 2)
    for v in range(variables):
        flat = cells[v].T
        state_out[v, :, 0:256] = flat[0:blocks]
        state_out[v, :, 256:512] = flat[blocks:lanes]
    layers = []
    for z in range(2):
        layer = coef_ref[0] * cells[0, pl.ds(z, 32, stride=8), :]
        for v in range(1, variables):
            layer = layer + coef_ref[v] * cells[v, pl.ds(z, 32, stride=8), :]
        layers.append(layer)
    turned = jnp.concatenate(layers + layers, axis=0).T
    for z in range(2):
        for half in range(2):
            patch_out[:, pl.ds(64 * z + 32 * half, 32)] = turned[
                blocks * half : blocks * half + blocks, 32 * z : 32 * z + 32
            ]
    for step in range(STEPS):
        for direction in range(3):
            left(step, direction)


def advance(state_in, flux_derivative_matrices, speeds, rate_block, local_index, parallel_flow_coefficients):
    variables, blocks = state_in.shape[0], state_in.shape[1]
    lanes = 2 * blocks
    here = jnp.where(
        local_index >= 0, local_index // blocks * lanes + local_index % blocks, -1
    ).T
    right = jnp.where(here >= 0, here + blocks, -1)
    target = jnp.concatenate(
        [
            jnp.concatenate([right[0:1], here[1:2]], axis=1),
            jnp.concatenate([here[2:6], right[2:6]], axis=1),
            jnp.full((3, lanes), -1, jnp.int32),
        ],
        axis=0,
    )
    rate = jnp.tile(rate_block, 2)[None, :]
    vmem, smem = pl.BlockSpec(memory_space=pltpu.VMEM), pl.BlockSpec(memory_space=pltpu.SMEM)
    whole = (variables, 256, lanes)
    faces = (STEPS, 3, 64 * variables, lanes)
    pairs = pltpu.SemaphoreType.DMA((STEPS, 3))
    return pl.pallas_call(
        halo_kernel,
        out_shape=(
            jax.ShapeDtypeStruct(state_in.shape, jnp.float32),
            jax.ShapeDtypeStruct((blocks, 128), jnp.float32),
        ),
        in_specs=[vmem, smem, smem, smem, vmem, vmem],
        out_specs=(vmem, vmem),
        scratch_shapes=[
            pltpu.VMEM(whole, jnp.float32),
            pltpu.VMEM(whole, jnp.float32),
            pltpu.VMEM(whole, jnp.float32),
            pltpu.VMEM(whole, jnp.float32),
            pltpu.VMEM(faces, jnp.float32),
            pltpu.VMEM(faces, jnp.float32),
            pltpu.VMEM(faces, jnp.float32),
            pltpu.VMEM((5, 3 * lanes, lanes), jnp.bfloat16),
            pairs,
            pairs,
            pairs,
            pairs,
        ],
        compiler_params=pltpu.CompilerParams(
            collective_id=0, has_side_effects=True, vmem_limit_bytes=48 * 1024 * 1024
        ),
    )(
        state_in,
        0.5 * flux_derivative_matrices.reshape(-1),
        0.5 * speeds,
        parallel_flow_coefficients,
        rate,
        target,
    )


def fourier_tables(orders):
    longitudes = jnp.arange(NLON, dtype=jnp.int32)
    phase_index = longitudes[:, None] * orders[None, :] % NLON
    angle_rad = phase_index.astype(jnp.float32) * (2.0 * math.pi / NLON)
    return (jnp.cos(angle_rad), jnp.sin(angle_rad))


def legendre_start(sine_lat, orders):
    series_k = jnp.arange(1, DEGREES, dtype=jnp.int32).astype(jnp.float32)
    log_sums = jnp.concatenate(
        [
            jnp.zeros((1,), jnp.float32),
            jnp.cumsum(0.5 * jnp.log((2.0 * series_k + 1.0) / (2.0 * series_k))),
        ]
    )
    log_base = jnp.take(log_sums, orders)
    order_real = orders.astype(jnp.float32)
    return jnp.exp(
        0.5 * math.log(0.5) + log_base[None, :] + order_real[None, :] * jnp.log(sine_lat)[:, None]
    )


def pair_kernel(share_rows, start_ref, order_ref, cosine_ref, weight_ref, out_ref, table):
    diagonal = start_ref[...]
    height, pieces = diagonal.shape[0], diagonal.shape[1] // 128
    order = order_ref[...]
    square = order * order
    cosine = cosine_ref[...]

    def one_degree(degree, carried):
        previous, before = carried
        real = degree.astype(jnp.float32)
        top = jnp.full(diagonal.shape, 4.0 * real * real - 1.0, jnp.float32)
        lower = real - 1.0
        low = jnp.full(diagonal.shape, 4.0 * lower * lower - 1.0, jnp.float32)
        up = jnp.sqrt(jnp.maximum(top, 1.0) / jnp.maximum(real * real - square, 1.0))
        back = jnp.sqrt(jnp.maximum(lower * lower - square, 0.0) / jnp.maximum(low, 1.0))
        present = (up * cosine) * previous + (-up * back) * before
        present = present + jnp.where(order == real, diagonal, 0.0)
        at = pl.multiple_of(degree * height, height)
        for piece in range(pieces):
            table[piece, pl.ds(at, height), :] = present[:, 128 * piece : 128 * (piece + 1)]
        return present, previous

    zero = diagonal * 0.0
    lax.fori_loop(0, DEGREES, one_degree, (zero, zero), unroll=8)
    degrees = lax.broadcasted_iota(jnp.int32, (DEGREES, 1), 0).astype(jnp.float32)
    gain = POT_GAIN / (degrees * (degrees + 1.0) + KAPPA2)
    for row in range(share_rows):
        rows = jnp.concatenate(
            [table[piece, pl.ds(row, DEGREES, stride=height), :] for piece in range(pieces)], axis=1
        )
        out_ref[row] = lax.dot_general(
            rows * weight_ref[...],
            rows * gain,
            (((0,), (0,)), ((), ())),
            precision=HIGHEST_PRECISION,
            preferred_element_type=jnp.float32,
        )


def order_pairs(sine_lat, cosine_lat, weights_lat, orders):
    lat_total, share = sine_lat.shape[0], orders.shape[0]
    side = max(1, min(share, 128 // lat_total))
    share_rows, lanes = share // side, side * lat_total
    start = legendre_start(sine_lat, orders).T.reshape(side, share_rows, lat_total)
    start = jnp.swapaxes(start, 0, 1).reshape(share_rows, lanes)
    order_real = jnp.broadcast_to(
        orders.astype(jnp.float32).reshape(side, share_rows, 1), (side, share_rows, lat_total)
    )
    order_real = jnp.swapaxes(order_real, 0, 1).reshape(share_rows, lanes)
    height = -(-share_rows // 8) * 8
    start = jnp.pad(start, ((0, height - share_rows), (0, 0)))
    order_real = jnp.pad(order_real, ((0, height - share_rows), (0, 0)))
    cosine = jnp.tile(cosine_lat, side)[None, :]
    weight = jnp.tile(weights_lat, side)[None, :]
    pairs = pl.pallas_call(
        functools.partial(pair_kernel, share_rows),
        out_shape=jax.ShapeDtypeStruct((share_rows, lanes, lanes), jnp.float32),
        scratch_shapes=[pltpu.VMEM((lanes // 128, DEGREES * height, 128), jnp.float32)],
        compiler_params=pltpu.CompilerParams(vmem_limit_bytes=48 * 1024 * 1024),
    )(start, order_real, cosine, weight)
    blocks = [
        pairs[:, lat_total * at : lat_total * (at + 1), lat_total * at : lat_total * (at + 1)]
        for at in range(side)
    ]
    return jnp.concatenate(blocks, axis=0)


def solve_spectral(coef_re, coef_im, cosine_lat, sine_lat, weights_lat, orders):
    pairs = order_pairs(sine_lat, cosine_lat, weights_lat, orders)
    both = jnp.stack([coef_re.T, coef_im.T], axis=1)
    synth = jnp.einsum("rcj,rjk->crk", both, pairs, precision=HIGHEST_PRECISION)
    return (synth[0].T, synth[1].T)


def body(
    invariant_fluid_quantities,
    flux_derivative_matrices,
    levels,
    neighbours,
    block_latitude_band,
    block_longitude_segment,
    parallel_flow_coefficients,
):
    grp_size = lax.axis_size("grp")
    core_size = lax.axis_size("cores")
    device_total = grp_size * core_size
    block_portion = invariant_fluid_quantities.shape[1]
    device = lax.axis_index("grp") * core_size + lax.axis_index("cores")
    has_prev, has_next = device > 0, device < total - 1
    prev_id = (lax.div(device - 1, core_size), lax.rem(device - 1 + core_size, core_size))
    next_id = (lax.div(device + 1, core_size), lax.rem(device + 1, core_size))
    mesh_type = pl.DeviceIdType.MESH
    barrier = pltpu.get_barrier_semaphore()

    @pl.when(has_prev)
    def _():
        pl.semaphore_signal(barrier, inc=1, device_id=prev_id, device_id_type=mesh_type)

    @pl.when(has_next)
    def _():
        pl.semaphore_signal(barrier, inc=1, device_id=next_id, device_id_type=mesh_type)

    @pl.when(jnp.logical_not(has_prev))
    def _():
        before[...] = jnp.zeros_like(before)

    @pl.when(jnp.logical_not(has_next))
    def _():
        after[...] = jnp.zeros_like(after)

    left_half = lax.broadcasted_iota(jnp.int32, (1, lanes), 1) < blocks
    for v in range(variables):
        both = jnp.concatenate([state_ref[v, :, 0:256], state_ref[v, :, 256:512]], axis=0)
        cells[v] = both.T

    def copies(step, direction):
        to_prev = pltpu.make_async_remote_copy(
            src_ref=own.at[step, direction], dst_ref=after.at[step, direction],
            send_sem=send_prev.at[step, direction], recv_sem=recv_next.at[step, direction],
            device_id=prev_id, device_id_type=mesh_type,
        )
        to_next = pltpu.make_async_remote_copy(
            src_ref=own.at[step, direction], dst_ref=before.at[step, direction],
            send_sem=send_next.at[step, direction], recv_sem=recv_prev.at[step, direction],
            device_id=next_id, device_id_type=mesh_type,
        )
        return to_prev, to_next

    def start(step, direction):
        to_prev, to_next = copies(step, direction)

        @pl.when(has_prev)
        def _():
            to_prev.start()

        @pl.when(has_next)
        def _():
            to_next.start()

    def arrive(step, direction):
        to_prev, to_next = copies(step, direction)

        @pl.when(has_prev)
        def _():
            to_next.wait_recv()

        @pl.when(has_next)
        def _():
            to_prev.wait_recv()

    def left(step, direction):
        to_prev, to_next = copies(step, direction)

        @pl.when(has_prev)
        def _():
            to_prev.wait_send()

        @pl.when(has_next)
        def _():
            to_next.wait_send()

    def fill(step, direction):
        for v in range(variables):
            if direction == 0:
                own[step, 0, pl.ds(64 * v, 64), :] = jnp.where(
                    left_half, cells[v, 0:64, :], cells[v, 192:256, :]
                )
            elif direction == 1:
                for side in range(2):
                    for x in range(4):
                        own[step, 1, pl.ds(256 * side + 32 * v + 8 * x, 8), :] = cells[
                            v, pl.ds(64 * x + 56 * side, 8), :
                        ]
            else:
                for side in range(2):
                    own[step, 2, pl.ds(256 * side + 32 * v, 32), :] = cells[
                        v, pl.ds(7 * side, 32, stride=8), :
                    ]

    def gathered(step, direction, first, rows, face):
        part = pl.ds(first, rows)
        table = jnp.concatenate(
            [before[step, direction, part, :], own[step, direction, part, :], after[step, direction, part, :]],
            axis=1,
        )
        return split_dot(table, picks[face])

    def keep(v, at, rows, lower, upper, here):
        diffs[v, pl.ds(at, rows), :] = upper - lower
        laps[v, pl.ds(at, rows), :] = upper - 2.0 * here + lower

    def sides(step, direction):
        if direction == 0:
            known = target_ref[0:1, :] >= 0
            ghosts = gathered(step, 0, 0, 64 * variables, 0)
            for v in range(variables):
                ghost = jnp.where(known, ghosts[64 * v : 64 * v + 64], own[step, 0, pl.ds(64 * v, 64), :])
                slabs = [cells[v, pl.ds(64 * x, 64), :] for x in range(4)]
                first = jnp.where(left_half, ghost, pltpu.roll(slabs[3], blocks, 1))
                last = jnp.where(left_half, pltpu.roll(slabs[0], blocks, 1), ghost)
                line = [first] + slabs + [last]
                for x in range(4):
                    keep(v, 64 * x, 64, line[x], line[x + 2], slabs[x])
            return
        near, far = 2 * direction - 1, 2 * direction
        rows = 32 * variables
        low = gathered(step, direction, rows, rows, near)
        high = gathered(step, direction, 0, rows, far)
        know_low, know_high = target_ref[near : near + 1, :] >= 0, target_ref[far : far + 1, :] >= 0
        for v in range(variables):
            part = slice(32 * v, 32 * v + 32)
            low_v = jnp.where(know_low, low[part], own[step, direction, pl.ds(32 * v, 32), :])
            high_v = jnp.where(know_high, high[part], own[step, direction, pl.ds(rows + 32 * v, 32), :])
            if direction == 1:
                for x in range(4):
                    slab = cells[v, pl.ds(64 * x, 64), :]
                    lower = jnp.concatenate([low_v[8 * x : 8 * x + 8], slab[0:56]], axis=0)
                    upper = jnp.concatenate([slab[8:64], high_v[8 * x : 8 * x + 8]], axis=0)
                    keep(v, 64 * x, 64, lower, upper, slab)
            else:
                whole = cells[v].reshape(32, 8, lanes)
                height = lax.broadcasted_iota(jnp.int32, (32, 8, lanes), 1)
                lower = jnp.where(height == 0, low_v[:, None, :], pltpu.roll(whole, 1, 1))
                upper = jnp.where(height == 7, high_v[:, None, :], pltpu.roll(whole, 7, 1))
                keep(v, 0, 256, lower.reshape(256, lanes), upper.reshape(256, lanes), cells[v])

    def mix(direction, final):
        rows = 16

        def one_chunk(chunk, carry):
            part = pl.ds(pl.multiple_of(chunk * rows, rows), rows)
            steps = [diffs[v, part, :] for v in range(variables)]
            for i in range(variables):
                total_i = -speed_ref[direction] * laps[i, part, :]
                for j in range(variables):
                    total_i = total_i + flux_ref[(direction * variables + i) * variables + j] * steps[j]
                if direction > 0:
                    total_i = total_i + change[i, part, :]
                if final:
                    cells[i, part, :] = cells[i, part, :] - rate_ref[0:1, :] * total_i
                else:
                    change[i, part, :] = total_i
            return carry

        lax.fori_loop(0, 256 // rows, one_chunk, 0)

    fill(0, 0)

    pl.semaphore_wait(barrier, has_prev.astype(jnp.int32) + has_next.astype(jnp.int32))
    for step in range(STEPS):
        for direction in range(3):
            if step > 0 or direction > 0:
                fill(step, direction)
            start(step, direction)
        if step == 0:
            row_ids = lax.broadcasted_iota(jnp.int32, (3 * lanes, lanes), 0)
            for face in range(5):
                hit = row_ids == target_ref[face : face + 1, :]
                picks[face] = hit.astype(jnp.float32).astype(jnp.bfloat16)
        for direction in range(3):
            arrive(step, direction)
            sides(step, direction)
            mix(direction, direction == 2)
    for v in range(variables):
        flat = cells[v].T
        state_out[v, :, 0:256] = flat[0:blocks]
        state_out[v, :, 256:512] = flat[blocks:lanes]
    layers = []
    for z in range(2):
        layer = coef_ref[0] * cells[0, pl.ds(z, 32, stride=8), :]
        for v in range(1, variables):
            layer = layer + coef_ref[v] * cells[v, pl.ds(z, 32, stride=8), :]
        layers.append(layer)
    turned = jnp.concatenate(layers + layers, axis=0).T
    for z in range(2):
        for half in range(2):
            patch_out[:, pl.ds(64 * z + 32 * half, 32)] = turned[
                blocks * half : blocks * half + blocks, 32 * z : 32 * z + 32
            ]
    for step in range(STEPS):
        for direction in range(3):
            left(step, direction)


def advance(state_in, flux_derivative_matrices, speeds, rate_block, local_index, parallel_flow_coefficients):
    variables, blocks = state_in.shape[0], state_in.shape[1]
    lanes = 2 * blocks
    here = jnp.where(
        local_index >= 0, local_index // blocks * lanes + local_index % blocks, -1
    ).T
    right = jnp.where(here >= 0, here + blocks, -1)
    target = jnp.concatenate(
        [
            jnp.concatenate([right[0:1], here[1:2]], axis=1),
            jnp.concatenate([here[2:6], right[2:6]], axis=1),
            jnp.full((3, lanes), -1, jnp.int32),
        ],
        axis=0,
    )
    rate = jnp.tile(rate_block, 2)[None, :]
    vmem, smem = pl.BlockSpec(memory_space=pltpu.VMEM), pl.BlockSpec(memory_space=pltpu.SMEM)
    whole = (variables, 256, lanes)
    faces = (STEPS, 3, 64 * variables, lanes)
    pairs = pltpu.SemaphoreType.DMA((STEPS, 3))
    return pl.pallas_call(
        halo_kernel,
        out_shape=(
            jax.ShapeDtypeStruct(state_in.shape, jnp.float32),
            jax.ShapeDtypeStruct((blocks, 128), jnp.float32),
        ),
        in_specs=[vmem, smem, smem, smem, vmem, vmem],
        out_specs=(vmem, vmem),
        scratch_shapes=[
            pltpu.VMEM(whole, jnp.float32),
            pltpu.VMEM(whole, jnp.float32),
            pltpu.VMEM(whole, jnp.float32),
            pltpu.VMEM(whole, jnp.float32),
            pltpu.VMEM(faces, jnp.float32),
            pltpu.VMEM(faces, jnp.float32),
            pltpu.VMEM(faces, jnp.float32),
            pltpu.VMEM((5, 3 * lanes, lanes), jnp.bfloat16),
            pairs,
            pairs,
            pairs,
            pairs,
        ],
        compiler_params=pltpu.CompilerParams(
            collective_id=0, has_side_effects=True, vmem_limit_bytes=48 * 1024 * 1024
        ),
    )(
        state_in,
        0.5 * flux_derivative_matrices.reshape(-1),
        0.5 * speeds,
        parallel_flow_coefficients,
        rate,
        target,
    )


def fourier_tables(orders):
    longitudes = jnp.arange(NLON, dtype=jnp.int32)
    phase_index = longitudes[:, None] * orders[None, :] % NLON
    angle_rad = phase_index.astype(jnp.float32) * (2.0 * math.pi / NLON)
    return (jnp.cos(angle_rad), jnp.sin(angle_rad))


def legendre_start(sine_lat, orders):
    series_k = jnp.arange(1, DEGREES, dtype=jnp.int32).astype(jnp.float32)
    log_sums = jnp.concatenate(
        [
            jnp.zeros((1,), jnp.float32),
            jnp.cumsum(0.5 * jnp.log((2.0 * series_k + 1.0) / (2.0 * series_k))),
        ]
    )
    log_base = jnp.take(log_sums, orders)
    order_real = orders.astype(jnp.float32)
    return jnp.exp(
        0.5 * math.log(0.5) + log_base[None, :] + order_real[None, :] * jnp.log(sine_lat)[:, None]
    )


def pair_kernel(share_rows, start_ref, order_ref, cosine_ref, weight_ref, out_ref, table):
    diagonal = start_ref[...]
    height, pieces = diagonal.shape[0], diagonal.shape[1] // 128
    order = order_ref[...]
    square = order * order
    cosine = cosine_ref[...]

    def one_degree(degree, carried):
        previous, before = carried
        real = degree.astype(jnp.float32)
        top = jnp.full(diagonal.shape, 4.0 * real * real - 1.0, jnp.float32)
        lower = real - 1.0
        low = jnp.full(diagonal.shape, 4.0 * lower * lower - 1.0, jnp.float32)
        up = jnp.sqrt(jnp.maximum(top, 1.0) / jnp.maximum(real * real - square, 1.0))
        back = jnp.sqrt(jnp.maximum(lower * lower - square, 0.0) / jnp.maximum(low, 1.0))
        present = (up * cosine) * previous + (-up * back) * before
        present = present + jnp.where(order == real, diagonal, 0.0)
        at = pl.multiple_of(degree * height, height)
        for piece in range(pieces):
            table[piece, pl.ds(at, height), :] = present[:, 128 * piece : 128 * (piece + 1)]
        return present, previous

    zero = diagonal * 0.0
    lax.fori_loop(0, DEGREES, one_degree, (zero, zero), unroll=8)
    degrees = lax.broadcasted_iota(jnp.int32, (DEGREES, 1), 0).astype(jnp.float32)
    gain = POT_GAIN / (degrees * (degrees + 1.0) + KAPPA2)
    for row in range(share_rows):
        rows = jnp.concatenate(
            [table[piece, pl.ds(row, DEGREES, stride=height), :] for piece in range(pieces)], axis=1
        )
        out_ref[row] = lax.dot_general(
            rows * weight_ref[...],
            rows * gain,
            (((0,), (0,)), ((), ())),
            precision=HIGHEST_PRECISION,
            preferred_element_type=jnp.float32,
        )


def order_pairs(sine_lat, cosine_lat, weights_lat, orders):
    lat_total, share = sine_lat.shape[0], orders.shape[0]
    side = max(1, min(share, 128 // lat_total))
    share_rows, lanes = share // side, side * lat_total
    start = legendre_start(sine_lat, orders).T.reshape(side, share_rows, lat_total)
    start = jnp.swapaxes(start, 0, 1).reshape(share_rows, lanes)
    order_real = jnp.broadcast_to(
        orders.astype(jnp.float32).reshape(side, share_rows, 1), (side, share_rows, lat_total)
    )
    order_real = jnp.swapaxes(order_real, 0, 1).reshape(share_rows, lanes)
    height = -(-share_rows // 8) * 8
    start = jnp.pad(start, ((0, height - share_rows), (0, 0)))
    order_real = jnp.pad(order_real, ((0, height - share_rows), (0, 0)))
    cosine = jnp.tile(cosine_lat, side)[None, :]
    weight = jnp.tile(weights_lat, side)[None, :]
    pairs = pl.pallas_call(
        functools.partial(pair_kernel, share_rows),
        out_shape=jax.ShapeDtypeStruct((share_rows, lanes, lanes), jnp.float32),
        scratch_shapes=[pltpu.VMEM((lanes // 128, DEGREES * height, 128), jnp.float32)],
        compiler_params=pltpu.CompilerParams(vmem_limit_bytes=48 * 1024 * 1024),
    )(start, order_real, cosine, weight)
    blocks = [
        pairs[:, lat_total * at : lat_total * (at + 1), lat_total * at : lat_total * (at + 1)]
        for at in range(side)
    ]
    return jnp.concatenate(blocks, axis=0)


def solve_spectral(coef_re, coef_im, cosine_lat, sine_lat, weights_lat, orders):
    pairs = order_pairs(sine_lat, cosine_lat, weights_lat, orders)
    both = jnp.stack([coef_re.T, coef_im.T], axis=1)
    synth = jnp.einsum("rcj,rjk->crk", both, pairs, precision=HIGHEST_PRECISION)
    return (synth[0].T, synth[1].T)


def body(
    invariant_fluid_quantities,
    flux_derivative_matrices,
    levels,
    neighbours,
    block_latitude_band,
    block_longitude_segment,
    parallel_flow_coefficients,
):
    grp_size = lax.axis_size("grp")
    core_size = lax.axis_size("cores")
    device_total = grp_size * core_size
    block_portion = invariant_fluid_quantities.shape[1]
    state_variables = invariant_fluid_quantities.shape[0]
    device = lax.axis_index(("grp", "cores"))
    speeds = wave_speeds(flux_derivative_matrices)
    rate_block = COURANT * jnp.exp2(levels.astype(jnp.float32) - (LEVELS - 1)) / jnp.max(speeds)
    offset = (device - 1) * block_portion
    local_index = jnp.where(neighbours >= 0, neighbours - offset, -1)
    parallel_flow_charge, patches = advance(
        invariant_fluid_quantities,
        flux_derivative_matrices,
        speeds,
        rate_block,
        local_index,
        parallel_flow_coefficients,
    )
    band_index = block_latitude_band[:, 0]
    block_ids = jnp.arange(block_portion, dtype=jnp.int32)
    earlier = (band_index[None, :] == band_index[:, None]) & (
        block_ids[None, :] < block_ids[:, None]
    )
    rank_in_band = jnp.sum(earlier.astype(jnp.int32), axis=1)
    capacity = max(2, 2 * block_portion // grp_size)
    slot_index = band_index * capacity + rank_in_band
    slot_ids = jnp.arange(grp_size * capacity, dtype=jnp.int32)
    placing = (slot_ids[:, None] == slot_index[None, :]).astype(jnp.float32)
    send_rows = jnp.dot(placing, patches, precision=HIGHEST_PRECISION).reshape(
        grp_size, capacity, 128
    )
    send_codes = jnp.dot(
        placing, (block_longitude_segment + 1).astype(jnp.float32), precision=HIGHEST_PRECISION
    ).reshape(grp_size, capacity)
    got_rows, got_codes = (
        lax.all_to_all(send_rows, "grp", split_axis=0, concat_axis=0, tiled=True),
        lax.all_to_all(send_codes, "grp", split_axis=0, concat_axis=0, tiled=True),
    )
    segments = NLON // 64
    segment_codes = jnp.arange(1, segments + 1, dtype=jnp.int32).astype(jnp.float32)
    landing = (got_codes.reshape(-1)[:, None] == segment_codes[None, :]).astype(jnp.float32)
    gathered = jnp.dot(landing.T, got_rows.reshape(-1, 128), precision=HIGHEST_PRECISION)
    fac_local = jnp.swapaxes(gathered.reshape(segments, LAT_DEV, 64), 0, 1).reshape(LAT_DEV, NLON)
    orders_all = jnp.arange(DEGREES, dtype=jnp.int32)
    cos_table, sin_table = fourier_tables(orders_all)
    coef_re = jnp.dot(fac_local, cos_table, precision=HIGHEST_PRECISION) / NLON
    coef_im = -jnp.dot(fac_local, sin_table, precision=HIGHEST_PRECISION) / NLON
    lat_total = LAT_DEV * device_total
    degree_share = DEGREES // device_total
    lat_ids = jnp.arange(lat_total, dtype=jnp.int32)
    colatitude = (lat_ids.astype(jnp.float32) + 0.5) * (math.pi / lat_total)
    cosine_all = jnp.cos(colatitude)
    sine_all = jnp.sin(colatitude)
    weights_all = math.pi / lat_total * sine_all
    own_orders = device * degree_share + jnp.arange(degree_share, dtype=jnp.int32)
    stacked = jnp.stack([coef_re, coef_im])
    regrouped = lax.all_to_all(
        lax.all_to_all(stacked, "grp", split_axis=2, concat_axis=1, tiled=True),
        "cores",
        split_axis=2,
        concat_axis=1,
        tiled=True,
    )
    regrouped = jnp.transpose(
        regrouped.reshape(2, core_size, grp_size, LAT_DEV, degree_share), (0, 2, 1, 3, 4)
    ).reshape(2, lat_total, degree_share)
    synth_re, synth_im = solve_spectral(
        regrouped[0], regrouped[1], cosine_all, sine_all, weights_all, own_orders
    )
    synth_both = jnp.stack([synth_re, synth_im])
    returned = lax.all_to_all(
        lax.all_to_all(synth_both, "grp", split_axis=1, concat_axis=2, tiled=True),
        "cores",
        split_axis=1,
        concat_axis=2,
        tiled=True,
    )
    column_ids = jnp.arange(DEGREES, dtype=jnp.int32)
    order_perm = (
        degree_share
        * (
            core_size * (column_ids // degree_share % grp_size)
            + column_ids // (grp_size * degree_share)
        )
        + column_ids % degree_share
    )
    cos_perm, sin_perm = fourier_tables(order_perm)
    factor = jnp.where(order_perm == 0, jnp.float32(1.0), jnp.float32(2.0))
    potential_local = jnp.dot(
        returned[0] * factor, cos_perm.T, precision=HIGHEST_PRECISION
    ) - jnp.dot(returned[1] * factor, sin_perm.T, precision=HIGHEST_PRECISION)
    grid_segments = jnp.swapaxes(potential_local.reshape(LAT_DEV, segments, 64), 0, 1).reshape(
        segments, 128
    )
    back_rows = jnp.dot(landing, grid_segments, precision=HIGHEST_PRECISION).reshape(
        grp_size, capacity, 128
    )
    home_rows = lax.all_to_all(back_rows, "grp", split_axis=0, concat_axis=0, tiled=True)
    shell_potential = jnp.dot(placing.T, home_rows.reshape(-1, 128), precision=HIGHEST_PRECISION)
    return (parallel_flow_charge, fac_local, potential_local, shell_potential)


def solution(mesh):
    placed = (
        P(None, ("grp", "cores"), None),
        P(),
        P(("grp", "cores")),
        P(("grp", "cores"), None),
        P(("grp", "cores"), None),
        P(("grp", "cores")),
        P(),
    )
    return jax.shard_map(
        body,
        mesh=mesh,
        in_specs=placed,
        out_specs=(
            P(None, ("grp", "cores"), None),
            P(("grp", "cores"), None),
            P(("grp", "cores"), None),
            P(("grp", "cores"), None),
        ),
        check_vma=False,
    )
```

```python
import functools
import math

import jax
import jax.numpy as jnp
import numpy as np
from jax import lax
from jax.experimental import pallas as pl
from jax.experimental.pallas import tpu as pltpu
from jax.sharding import PartitionSpec as P

LEVELS = 4
STEPS = 2
LAT_DEV = 2
NLON = 1024
DEGREES = 512


COURANT = 0.3
KAPPA2 = 400.0
POT_GAIN = 2000.0
HIGHEST_PRECISION = lax.Precision.HIGHEST


def wave_speeds(flux_derivative_matrices):
    return jnp.max(jnp.sum(jnp.abs(flux_derivative_matrices), axis=2), axis=1)


def split_dot(values, picks):
    high = values.astype(jnp.bfloat16)
    low = (values - high.astype(jnp.float32)).astype(jnp.bfloat16)
    return jnp.dot(high, picks, preferred_element_type=jnp.float32) + jnp.dot(
        low, picks, preferred_element_type=jnp.float32
    )


def halo_kernel(
    state_ref, flux_ref, speed_ref, coef_ref, rate_ref, target_ref,
    state_out, patch_out,
    cells, diffs, laps, change, own, before, after, picks,
    send_prev, send_next, recv_prev, recv_next,
):
    variables, blocks = state_ref.shape[0], state_ref.shape[1]
    lanes = 2 * blocks
    core_size = lax.axis_size("cores")
    total = lax.axis_size("grp") * core_size
    device = lax.axis_index("grp") * core_size + lax.axis_index("cores")
    has_prev, has_next = device > 0, device < total - 1
    prev_id = (lax.div(device - 1, core_size), lax.rem(device - 1 + core_size, core_size))
    next_id = (lax.div(device + 1, core_size), lax.rem(device + 1, core_size))
    mesh_type = pl.DeviceIdType.MESH
    barrier = pltpu.get_barrier_semaphore()

    @pl.when(has_prev)
    def _():
        pl.semaphore_signal(barrier, inc=1, device_id=prev_id, device_id_type=mesh_type)

    @pl.when(has_next)
    def _():
        pl.semaphore_signal(barrier, inc=1, device_id=next_id, device_id_type=mesh_type)

    @pl.when(jnp.logical_not(has_prev))
    def _():
        before[...] = jnp.zeros_like(before)

    @pl.when(jnp.logical_not(has_next))
    def _():
        after[...] = jnp.zeros_like(after)

    left_half = lax.broadcasted_iota(jnp.int32, (1, lanes), 1) < blocks
    for v in range(variables):
        both = jnp.concatenate([state_ref[v, :, 0:256], state_ref[v, :, 256:512]], axis=0)
        cells[v] = both.T

    def copies(step, direction):
        to_prev = pltpu.make_async_remote_copy(
            src_ref=own.at[step, direction], dst_ref=after.at[step, direction],
            send_sem=send_prev.at[step, direction], recv_sem=recv_next.at[step, direction],
            device_id=prev_id, device_id_type=mesh_type,
        )
        to_next = pltpu.make_async_remote_copy(
            src_ref=own.at[step, direction], dst_ref=before.at[step, direction],
            send_sem=send_next.at[step, direction], recv_sem=recv_prev.at[step, direction],
            device_id=next_id, device_id_type=mesh_type,
        )
        return to_prev, to_next

    def start(step, direction):
        to_prev, to_next = copies(step, direction)

        @pl.when(has_prev)
        def _():
            to_prev.start()

        @pl.when(has_next)
        def _():
            to_next.start()

    def arrive(step, direction):
        to_prev, to_next = copies(step, direction)

        @pl.when(has_prev)
        def _():
            to_next.wait_recv()

        @pl.when(has_next)
        def _():
            to_prev.wait_recv()

    def left(step, direction):
        to_prev, to_next = copies(step, direction)

        @pl.when(has_prev)
        def _():
            to_prev.wait_send()

        @pl.when(has_next)
        def _():
            to_next.wait_send()

    def fill(step, direction):
        for v in range(variables):
            if direction == 0:
                own[step, 0, pl.ds(64 * v, 64), :] = jnp.where(
                    left_half, cells[v, 0:64, :], cells[v, 192:256, :]
                )
            elif direction == 1:
                for side in range(2):
                    for x in range(4):
                        own[step, 1, pl.ds(256 * side + 32 * v + 8 * x, 8), :] = cells[
                            v, pl.ds(64 * x + 56 * side, 8), :
                        ]
            else:
                for side in range(2):
                    own[step, 2, pl.ds(256 * side + 32 * v, 32), :] = cells[
                        v, pl.ds(7 * side, 32, stride=8), :
                    ]

    def gathered(step, direction, first, rows, face):
        part = pl.ds(first, rows)
        table = jnp.concatenate(
            [before[step, direction, part, :], own[step, direction, part, :], after[step, direction, part, :]],
            axis=1,
        )
        return split_dot(table, picks[face])

    def keep(v, at, rows, lower, upper, here):
        diffs[v, pl.ds(at, rows), :] = upper - lower
        laps[v, pl.ds(at, rows), :] = upper - 2.0 * here + lower

    def sides(step, direction):
        if direction == 0:
            known = target_ref[0:1, :] >= 0
            ghosts = gathered(step, 0, 0, 64 * variables, 0)
            for v in range(variables):
                ghost = jnp.where(known, ghosts[64 * v : 64 * v + 64], own[step, 0, pl.ds(64 * v, 64), :])
                slabs = [cells[v, pl.ds(64 * x, 64), :] for x in range(4)]
                first = jnp.where(left_half, ghost, pltpu.roll(slabs[3], blocks, 1))
                last = jnp.where(left_half, pltpu.roll(slabs[0], blocks, 1), ghost)
                line = [first] + slabs + [last]
                for x in range(4):
                    keep(v, 64 * x, 64, line[x], line[x + 2], slabs[x])
            return
        near, far = 2 * direction - 1, 2 * direction
        rows = 32 * variables
        low = gathered(step, direction, rows, rows, near)
        high = gathered(step, direction, 0, rows, far)
        know_low, know_high = target_ref[near : near + 1, :] >= 0, target_ref[far : far + 1, :] >= 0
        for v in range(variables):
            part = slice(32 * v, 32 * v + 32)
            low_v = jnp.where(know_low, low[part], own[step, direction, pl.ds(32 * v, 32), :])
            high_v = jnp.where(know_high, high[part], own[step, direction, pl.ds(rows + 32 * v, 32), :])
            if direction == 1:
                for x in range(4):
                    slab = cells[v, pl.ds(64 * x, 64), :]
                    lower = jnp.concatenate([low_v[8 * x : 8 * x + 8], slab[0:56]], axis=0)
                    upper = jnp.concatenate([slab[8:64], high_v[8 * x : 8 * x + 8]], axis=0)
                    keep(v, 64 * x, 64, lower, upper, slab)
            else:
                whole = cells[v].reshape(32, 8, lanes)
                height = lax.broadcasted_iota(jnp.int32, (32, 8, lanes), 1)
                lower = jnp.where(height == 0, low_v[:, None, :], pltpu.roll(whole, 1, 1))
                upper = jnp.where(height == 7, high_v[:, None, :], pltpu.roll(whole, 7, 1))
                keep(v, 0, 256, lower.reshape(256, lanes), upper.reshape(256, lanes), cells[v])

    def mix(direction, final):
        rows = 16

        def one_chunk(chunk, carry):
            part = pl.ds(pl.multiple_of(chunk * rows, rows), rows)
            steps = [diffs[v, part, :] for v in range(variables)]
            for i in range(variables):
                total_i = -speed_ref[direction] * laps[i, part, :]
                for j in range(variables):
                    total_i = total_i + flux_ref[(direction * variables + i) * variables + j] * steps[j]
                if direction > 0:
                    total_i = total_i + change[i, part, :]
                if final:
                    cells[i, part, :] = cells[i, part, :] - rate_ref[0:1, :] * total_i
                else:
                    change[i, part, :] = total_i
            return carry

        lax.fori_loop(0, 256 // rows, one_chunk, 0)

    fill(0, 0)

    pl.semaphore_wait(barrier, has_prev.astype(jnp.int32) + has_next.astype(jnp.int32))
    for step in range(STEPS):
        for direction in range(3):
            if step > 0 or direction > 0:
                fill(step, direction)
            start(step, direction)
        if step == 0:
            row_ids = lax.broadcasted_iota(jnp.int32, (3 * lanes, lanes), 0)
            for face in range(5):
                hit = row_ids == target_ref[face : face + 1, :]
                picks[face] = hit.astype(jnp.float32).astype(jnp.bfloat16)
        for direction in range(3):
            arrive(step, direction)
            sides(step, direction)
            mix(direction, direction == 2)
    for v in range(variables):
        flat = cells[v].T
        state_out[v, :, 0:256] = flat[0:blocks]
        state_out[v, :, 256:512] = flat[blocks:lanes]
    layers = []
    for z in range(2):
        layer = coef_ref[0] * cells[0, pl.ds(z, 32, stride=8), :]
        for v in range(1, variables):
            layer = layer + coef_ref[v] * cells[v, pl.ds(z, 32, stride=8), :]
        layers.append(layer)
    turned = jnp.concatenate(layers + layers, axis=0).T
    for z in range(2):
        for half in range(2):
            patch_out[:, pl.ds(64 * z + 32 * half, 32)] = turned[
                blocks * half : blocks * half + blocks, 32 * z : 32 * z + 32
            ]
    for step in range(STEPS):
        for direction in range(3):
            left(step, direction)


def advance(state_in, flux_derivative_matrices, speeds, rate_block, local_index, parallel_flow_coefficients):
    variables, blocks = state_in.shape[0], state_in.shape[1]
    lanes = 2 * blocks
    here = jnp.where(
        local_index >= 0, local_index // blocks * lanes + local_index % blocks, -1
    ).T
    right = jnp.where(here >= 0, here + blocks, -1)
    target = jnp.concatenate(
        [
            jnp.concatenate([right[0:1], here[1:2]], axis=1),
            jnp.concatenate([here[2:6], right[2:6]], axis=1),
            jnp.full((3, lanes), -1, jnp.int32),
        ],
        axis=0,
    )
    rate = jnp.tile(rate_block, 2)[None, :]
    vmem, smem = pl.BlockSpec(memory_space=pltpu.VMEM), pl.BlockSpec(memory_space=pltpu.SMEM)
    whole = (variables, 256, lanes)
    faces = (STEPS, 3, 64 * variables, lanes)
    pairs = pltpu.SemaphoreType.DMA((STEPS, 3))
    return pl.pallas_call(
        halo_kernel,
        out_shape=(
            jax.ShapeDtypeStruct(state_in.shape, jnp.float32),
            jax.ShapeDtypeStruct((blocks, 128), jnp.float32),
        ),
        in_specs=[vmem, smem, smem, smem, vmem, vmem],
        out_specs=(vmem, vmem),
        scratch_shapes=[
            pltpu.VMEM(whole, jnp.float32),
            pltpu.VMEM(whole, jnp.float32),
            pltpu.VMEM(whole, jnp.float32),
            pltpu.VMEM(whole, jnp.float32),
            pltpu.VMEM(faces, jnp.float32),
            pltpu.VMEM(faces, jnp.float32),
            pltpu.VMEM(faces, jnp.float32),
            pltpu.VMEM((5, 3 * lanes, lanes), jnp.bfloat16),
            pairs,
            pairs,
            pairs,
            pairs,
        ],
        compiler_params=pltpu.CompilerParams(
            collective_id=0, has_side_effects=True, vmem_limit_bytes=48 * 1024 * 1024
        ),
    )(
        state_in,
        0.5 * flux_derivative_matrices.reshape(-1),
        0.5 * speeds,
        parallel_flow_coefficients,
        rate,
        target,
    )


def legendre_start(sine_lat, orders):
    series_k = jnp.arange(1, DEGREES, dtype=jnp.int32).astype(jnp.float32)
    log_sums = jnp.concatenate(
        [
            jnp.zeros((1,), jnp.float32),
            jnp.cumsum(0.5 * jnp.log((2.0 * series_k + 1.0) / (2.0 * series_k))),
        ]
    )
    log_base = jnp.take(log_sums, orders)
    order_real = orders.astype(jnp.float32)
    return jnp.exp(
        0.5 * math.log(0.5) + log_base[None, :] + order_real[None, :] * jnp.log(sine_lat)[:, None]
    )


def pair_kernel(share_rows, start_ref, order_ref, cosine_ref, weight_ref, out_ref, table):
    diagonal = start_ref[...]
    height, pieces = diagonal.shape[0], diagonal.shape[1] // 128
    order = order_ref[...]
    square = order * order
    cosine = cosine_ref[...]

    def one_degree(degree, carried):
        previous, before = carried
        real = degree.astype(jnp.float32)
        top = jnp.full(diagonal.shape, 4.0 * real * real - 1.0, jnp.float32)
        lower = real - 1.0
        low = jnp.full(diagonal.shape, 4.0 * lower * lower - 1.0, jnp.float32)
        up = jnp.sqrt(jnp.maximum(top, 1.0) / jnp.maximum(real * real - square, 1.0))
        back = jnp.sqrt(jnp.maximum(lower * lower - square, 0.0) / jnp.maximum(low, 1.0))
        present = (up * cosine) * previous + (-up * back) * before
        present = present + jnp.where(order == real, diagonal, 0.0)
        at = pl.multiple_of(degree * height, height)
        for piece in range(pieces):
            table[piece, pl.ds(at, height), :] = present[:, 128 * piece : 128 * (piece + 1)]
        return present, previous

    zero = diagonal * 0.0
    lax.fori_loop(0, DEGREES, one_degree, (zero, zero), unroll=8)
    degrees = lax.broadcasted_iota(jnp.int32, (DEGREES, 1), 0).astype(jnp.float32)
    gain = POT_GAIN / (degrees * (degrees + 1.0) + KAPPA2)
    for row in range(share_rows):
        rows = jnp.concatenate(
            [table[piece, pl.ds(row, DEGREES, stride=height), :] for piece in range(pieces)], axis=1
        )
        out_ref[row] = lax.dot_general(
            rows * weight_ref[...],
            rows * gain,
            (((0,), (0,)), ((), ())),
            precision=HIGHEST_PRECISION,
            preferred_element_type=jnp.float32,
        )


def order_pairs(sine_lat, cosine_lat, weights_lat, orders):
    lat_total, share = sine_lat.shape[0], orders.shape[0]
    side = max(1, min(share, 128 // lat_total))
    share_rows, lanes = share // side, side * lat_total
    start = legendre_start(sine_lat, orders).T.reshape(side, share_rows, lat_total)
    start = jnp.swapaxes(start, 0, 1).reshape(share_rows, lanes)
    order_real = jnp.broadcast_to(
        orders.astype(jnp.float32).reshape(side, share_rows, 1), (side, share_rows, lat_total)
    )
    order_real = jnp.swapaxes(order_real, 0, 1).reshape(share_rows, lanes)
    height = -(-share_rows // 8) * 8
    start = jnp.pad(start, ((0, height - share_rows), (0, 0)))
    order_real = jnp.pad(order_real, ((0, height - share_rows), (0, 0)))
    cosine = jnp.tile(cosine_lat, side)[None, :]
    weight = jnp.tile(weights_lat, side)[None, :]
    pairs = pl.pallas_call(
        functools.partial(pair_kernel, share_rows),
        out_shape=jax.ShapeDtypeStruct((share_rows, lanes, lanes), jnp.float32),
        scratch_shapes=[pltpu.VMEM((lanes // 128, DEGREES * height, 128), jnp.float32)],
        compiler_params=pltpu.CompilerParams(vmem_limit_bytes=48 * 1024 * 1024),
    )(start, order_real, cosine, weight)
    blocks = [
        pairs[:, lat_total * at : lat_total * (at + 1), lat_total * at : lat_total * (at + 1)]
        for at in range(side)
    ]
    return jnp.concatenate(blocks, axis=0)


def exact_dot(left, right, contract):
    return lax.dot_general(
        left, right, (contract, ((), ())),
        precision=HIGHEST_PRECISION, preferred_element_type=jnp.float32,
    )


def wave_constants():
    order = np.arange(128) // 8
    used = (np.arange(128) % 8 < 2)[:, None]
    seg = 2.0 * np.pi / 16 * order[:, None] * np.arange(16)[None, :]
    turn = 2.0 * np.pi / NLON * order[:, None] * (np.arange(128) % 64)[None, :]
    high = 2.0 * np.pi / 64 * np.arange(DEGREES // 16)[:, None] * np.arange(64)[None, :]
    factor = np.full((DEGREES // 16, 128), 2.0)
    factor[0, :8] = 1.0
    listed = [np.cos(seg) * used, np.sin(seg) * used, np.cos(turn), np.sin(turn)]
    listed += [np.cos(high), np.sin(high), factor]
    return [jnp.asarray(one, jnp.float32) for one in listed]


def harmonic_kernel(
    share, message_ref, pairs_ref, seg_cos, seg_sin, turn_cos, turn_sin, high_cos, high_sin, factor_ref,
    grid_out, potential_out, home_out,
    got, coef_send, coef_got, waves, solved, synth_send, synth_got, back_send, home,
    send_a, recv_a, send_b, recv_b, send_c, recv_c, send_d, recv_d,
):
    core_size, groups = lax.axis_size("cores"), lax.axis_size("grp")
    total = core_size * groups
    group, core = lax.axis_index("grp"), lax.axis_index("cores")
    device = group * core_size + core
    mesh_type = pl.DeviceIdType.MESH
    barrier = pltpu.get_barrier_semaphore()

    def greet(k, carry):
        peer = lax.rem(device + k, total)
        pl.semaphore_signal(
            barrier, inc=1,
            device_id=(lax.div(peer, core_size), lax.rem(peer, core_size)), device_id_type=mesh_type,
        )
        return carry

    lax.fori_loop(1, total, greet, 0)

    def exchange(source, target, send, recv, over_all, pick):
        count, me = (total, device) if over_all else (groups, group)

        def copy(k):
            peer = lax.rem(me + k, count)
            where = (lax.div(peer, core_size), lax.rem(peer, core_size)) if over_all else (peer, core)
            return pltpu.make_async_remote_copy(
                src_ref=source.at[pick(peer)], dst_ref=target.at[me],
                send_sem=send.at[k], recv_sem=recv.at[k],
                device_id=where, device_id_type=mesh_type,
            )

        def begin(k, carry):
            copy(k).start()
            return carry

        def finish(k, carry):
            copy(k).wait_recv()
            return carry

        def drain(k, carry):
            copy(k).wait_send()
            return carry

        lax.fori_loop(1, count, begin, 0)
        target[me] = source[pick(me)]
        return lambda: lax.fori_loop(1, count, finish, 0), lambda: lax.fori_loop(1, count, drain, 0)

    same = lambda peer: peer
    pl.semaphore_wait(barrier, total - 1)
    arrived, drain_a = exchange(message_ref, got, send_a, recv_a, False, same)
    capacity = message_ref.shape[1] // 2
    slots = groups * capacity
    arrived()
    rows = got[:, 0:capacity, :].reshape(slots, 128)
    codes = got[:, capacity : 2 * capacity, :].reshape(slots, 128)
    seg_ids = lax.broadcasted_iota(jnp.int32, (slots, 128), 1).astype(jnp.float32) + 1.0
    landing = (codes == seg_ids).astype(jnp.float32)
    grid = exact_dot(landing, rows, ((0,), (0,)))[0:16]
    grid_out[...] = grid
    near_re = exact_dot(seg_cos[...], grid, ((1,), (0,)))
    near_im = -exact_dot(seg_sin[...], grid, ((1,), (0,)))
    mid_re = near_re * turn_cos[...] + near_im * turn_sin[...]
    mid_im = near_im * turn_cos[...] - near_re * turn_sin[...]
    real_row = lax.broadcasted_iota(jnp.int32, (128, 128), 0) % 8 == 0
    with_cos = jnp.where(real_row, mid_re, mid_im)
    with_sin = jnp.where(real_row, mid_im, -mid_re)
    for z in range(2):
        lat = slice(64 * z, 64 * z + 64)
        coef = exact_dot(high_cos[...], with_cos[:, lat], ((1,), (1,)))
        coef = coef + exact_dot(high_sin[...], with_sin[:, lat], ((1,), (1,)))
        coef_send[:, z, :] = coef / NLON
    arrived, drain_b = exchange(
        coef_send, coef_got, send_b, recv_b, True, lambda peer: lax.div(peer * share, 16)
    )
    arrived()
    cut = jnp.concatenate([coef_got[:, z, :].T for z in range(2)], axis=1)
    waves[...] = cut.reshape(16, 8, 2 * total)
    if share < 16:
        solved[...] = jnp.zeros_like(solved)
    first = lax.rem(share * device, 16)
    for order in range(share):
        solved[first + order] = exact_dot(waves[first + order], pairs_ref[order], ((1,), (0,)))
    back = solved[...].reshape(128, 2 * total).T
    for z in range(2):
        synth_send[:, z, :] = back[z * total : (z + 1) * total]
    arrived, drain_c = exchange(synth_send, synth_got, send_c, recv_c, True, same)
    arrived()
    parts_cos, parts_sin = [], []
    for z in range(2):
        part = synth_got[:, z, :]
        if total > DEGREES // 16:
            part = jnp.sum(part.reshape(DEGREES // 16, total * 16 // DEGREES, 128), axis=1)
        part = part * factor_ref[...]
        parts_cos.append(exact_dot(part, high_cos[...], ((0,), (0,))))
        parts_sin.append(exact_dot(part, high_sin[...], ((0,), (0,))))
    full_cos, full_sin = jnp.concatenate(parts_cos, axis=1), jnp.concatenate(parts_sin, axis=1)
    alpha = full_cos * turn_cos[...] - full_sin * turn_sin[...]
    beta = full_cos * turn_sin[...] + full_sin * turn_cos[...]
    potential = exact_dot(seg_cos[...], jnp.where(real_row, alpha, -beta), ((0,), (0,)))
    potential = potential - exact_dot(seg_sin[...], jnp.where(real_row, beta, alpha), ((0,), (0,)))
    potential_out[...] = potential
    spread = exact_dot(landing[:, 0:16], potential, ((1,), (0,)))
    back_send[...] = spread.reshape(groups, capacity, 128)
    arrived, drain_d = exchange(back_send, home, send_d, recv_d, False, same)
    arrived()
    home_out[...] = home[...]
    drain_a()
    drain_b()
    drain_c()
    drain_d()


def harmonic_solve(message, pairs, total):
    groups, capacity = message.shape[0], message.shape[1] // 2
    share = pairs.shape[0]
    wide = DEGREES // 16
    vmem = pl.BlockSpec(memory_space=pltpu.VMEM)
    few, many = pltpu.SemaphoreType.DMA((groups,)), pltpu.SemaphoreType.DMA((total,))
    room = lambda *shape: pltpu.VMEM(shape, jnp.float32)
    result = lambda *shape: jax.ShapeDtypeStruct(shape, jnp.float32)
    return pl.pallas_call(
        functools.partial(harmonic_kernel, share),
        out_shape=(result(16, 128), result(16, 128), result(groups, capacity, 128)),
        in_specs=[vmem] * 9,
        out_specs=(vmem, vmem, vmem),
        scratch_shapes=[
            room(groups, 2 * capacity, 128),
            room(wide, 8, 128),
            room(total, 8, 128),
            room(16, 8, 2 * total),
            room(16, 8, 2 * total),
            room(total, 8, 128),
            room(total, 8, 128),
            room(groups, capacity, 128),
            room(groups, capacity, 128),
            few, few, many, many, many, many, few, few,
        ],
        compiler_params=pltpu.CompilerParams(
            collective_id=1, has_side_effects=True, vmem_limit_bytes=48 * 1024 * 1024
        ),
    )(message, pairs, *wave_constants())


def body(
    invariant_fluid_quantities,
    flux_derivative_matrices,
    levels,
    neighbours,
    block_latitude_band,
    block_longitude_segment,
    parallel_flow_coefficients,
):
    grp_size = lax.axis_size("grp")
    core_size = lax.axis_size("cores")
    device_total = grp_size * core_size
    block_portion = invariant_fluid_quantities.shape[1]
    device = lax.axis_index("grp") * core_size + lax.axis_index("cores")
    has_prev, has_next = device > 0, device < total - 1
    prev_id = (lax.div(device - 1, core_size), lax.rem(device - 1 + core_size, core_size))
    next_id = (lax.div(device + 1, core_size), lax.rem(device + 1, core_size))
    mesh_type = pl.DeviceIdType.MESH
    barrier = pltpu.get_barrier_semaphore()

    @pl.when(has_prev)
    def _():
        pl.semaphore_signal(barrier, inc=1, device_id=prev_id, device_id_type=mesh_type)

    @pl.when(has_next)
    def _():
        pl.semaphore_signal(barrier, inc=1, device_id=next_id, device_id_type=mesh_type)

    @pl.when(jnp.logical_not(has_prev))
    def _():
        before[...] = jnp.zeros_like(before)

    @pl.when(jnp.logical_not(has_next))
    def _():
        after[...] = jnp.zeros_like(after)

    left_half = lax.broadcasted_iota(jnp.int32, (1, lanes), 1) < blocks
    for v in range(variables):
        both = jnp.concatenate([state_ref[v, :, 0:256], state_ref[v, :, 256:512]], axis=0)
        cells[v] = both.T

    def copies(step, direction):
        to_prev = pltpu.make_async_remote_copy(
            src_ref=own.at[step, direction], dst_ref=after.at[step, direction],
            send_sem=send_prev.at[step, direction], recv_sem=recv_next.at[step, direction],
            device_id=prev_id, device_id_type=mesh_type,
        )
        to_next = pltpu.make_async_remote_copy(
            src_ref=own.at[step, direction], dst_ref=before.at[step, direction],
            send_sem=send_next.at[step, direction], recv_sem=recv_prev.at[step, direction],
            device_id=next_id, device_id_type=mesh_type,
        )
        return to_prev, to_next

    def start(step, direction):
        to_prev, to_next = copies(step, direction)

        @pl.when(has_prev)
        def _():
            to_prev.start()

        @pl.when(has_next)
        def _():
            to_next.start()

    def arrive(step, direction):
        to_prev, to_next = copies(step, direction)

        @pl.when(has_prev)
        def _():
            to_next.wait_recv()

        @pl.when(has_next)
        def _():
            to_prev.wait_recv()

    def left(step, direction):
        to_prev, to_next = copies(step, direction)

        @pl.when(has_prev)
        def _():
            to_prev.wait_send()

        @pl.when(has_next)
        def _():
            to_next.wait_send()

    def fill(step, direction):
        for v in range(variables):
            if direction == 0:
                own[step, 0, pl.ds(64 * v, 64), :] = jnp.where(
                    left_half, cells[v, 0:64, :], cells[v, 192:256, :]
                )
            elif direction == 1:
                for side in range(2):
                    for x in range(4):
                        own[step, 1, pl.ds(256 * side + 32 * v + 8 * x, 8), :] = cells[
                            v, pl.ds(64 * x + 56 * side, 8), :
                        ]
            else:
                for side in range(2):
                    own[step, 2, pl.ds(256 * side + 32 * v, 32), :] = cells[
                        v, pl.ds(7 * side, 32, stride=8), :
                    ]

    def gathered(step, direction, first, rows, face):
        part = pl.ds(first, rows)
        table = jnp.concatenate(
            [before[step, direction, part, :], own[step, direction, part, :], after[step, direction, part, :]],
            axis=1,
        )
        return split_dot(table, picks[face])

    def keep(v, at, rows, lower, upper, here):
        diffs[v, pl.ds(at, rows), :] = upper - lower
        laps[v, pl.ds(at, rows), :] = upper - 2.0 * here + lower

    def sides(step, direction):
        if direction == 0:
            known = target_ref[0:1, :] >= 0
            ghosts = gathered(step, 0, 0, 64 * variables, 0)
            for v in range(variables):
                ghost = jnp.where(known, ghosts[64 * v : 64 * v + 64], own[step, 0, pl.ds(64 * v, 64), :])
                slabs = [cells[v, pl.ds(64 * x, 64), :] for x in range(4)]
                first = jnp.where(left_half, ghost, pltpu.roll(slabs[3], blocks, 1))
                last = jnp.where(left_half, pltpu.roll(slabs[0], blocks, 1), ghost)
                line = [first] + slabs + [last]
                for x in range(4):
                    keep(v, 64 * x, 64, line[x], line[x + 2], slabs[x])
            return
        near, far = 2 * direction - 1, 2 * direction
        rows = 32 * variables
        low = gathered(step, direction, rows, rows, near)
        high = gathered(step, direction, 0, rows, far)
        know_low, know_high = target_ref[near : near + 1, :] >= 0, target_ref[far : far + 1, :] >= 0
        for v in range(variables):
            part = slice(32 * v, 32 * v + 32)
            low_v = jnp.where(know_low, low[part], own[step, direction, pl.ds(32 * v, 32), :])
            high_v = jnp.where(know_high, high[part], own[step, direction, pl.ds(rows + 32 * v, 32), :])
            if direction == 1:
                for x in range(4):
                    slab = cells[v, pl.ds(64 * x, 64), :]
                    lower = jnp.concatenate([low_v[8 * x : 8 * x + 8], slab[0:56]], axis=0)
                    upper = jnp.concatenate([slab[8:64], high_v[8 * x : 8 * x + 8]], axis=0)
                    keep(v, 64 * x, 64, lower, upper, slab)
            else:
                whole = cells[v].reshape(32, 8, lanes)
                height = lax.broadcasted_iota(jnp.int32, (32, 8, lanes), 1)
                lower = jnp.where(height == 0, low_v[:, None, :], pltpu.roll(whole, 1, 1))
                upper = jnp.where(height == 7, high_v[:, None, :], pltpu.roll(whole, 7, 1))
                keep(v, 0, 256, lower.reshape(256, lanes), upper.reshape(256, lanes), cells[v])

    def mix(direction, final):
        rows = 16

        def one_chunk(chunk, carry):
            part = pl.ds(pl.multiple_of(chunk * rows, rows), rows)
            steps = [diffs[v, part, :] for v in range(variables)]
            for i in range(variables):
                total_i = -speed_ref[direction] * laps[i, part, :]
                for j in range(variables):
                    total_i = total_i + flux_ref[(direction * variables + i) * variables + j] * steps[j]
                if direction > 0:
                    total_i = total_i + change[i, part, :]
                if final:
                    cells[i, part, :] = cells[i, part, :] - rate_ref[0:1, :] * total_i
                else:
                    change[i, part, :] = total_i
            return carry

        lax.fori_loop(0, 256 // rows, one_chunk, 0)

    fill(0, 0)

    pl.semaphore_wait(barrier, has_prev.astype(jnp.int32) + has_next.astype(jnp.int32))
    for step in range(STEPS):
        for direction in range(3):
            if step > 0 or direction > 0:
                fill(step, direction)
            start(step, direction)
        if step == 0:
            row_ids = lax.broadcasted_iota(jnp.int32, (3 * lanes, lanes), 0)
            for face in range(5):
                hit = row_ids == target_ref[face : face + 1, :]
                picks[face] = hit.astype(jnp.float32).astype(jnp.bfloat16)
        for direction in range(3):
            arrive(step, direction)
            sides(step, direction)
            mix(direction, direction == 2)
    for v in range(variables):
        flat = cells[v].T
        state_out[v, :, 0:256] = flat[0:blocks]
        state_out[v, :, 256:512] = flat[blocks:lanes]
    layers = []
    for z in range(2):
        layer = coef_ref[0] * cells[0, pl.ds(z, 32, stride=8), :]
        for v in range(1, variables):
            layer = layer + coef_ref[v] * cells[v, pl.ds(z, 32, stride=8), :]
        layers.append(layer)
    turned = jnp.concatenate(layers + layers, axis=0).T
    for z in range(2):
        for half in range(2):
            patch_out[:, pl.ds(64 * z + 32 * half, 32)] = turned[
                blocks * half : blocks * half + blocks, 32 * z : 32 * z + 32
            ]
    for step in range(STEPS):
        for direction in range(3):
            left(step, direction)


def advance(state_in, flux_derivative_matrices, speeds, rate_block, local_index, parallel_flow_coefficients):
    variables, blocks = state_in.shape[0], state_in.shape[1]
    lanes = 2 * blocks
    here = jnp.where(
        local_index >= 0, local_index // blocks * lanes + local_index % blocks, -1
    ).T
    right = jnp.where(here >= 0, here + blocks, -1)
    target = jnp.concatenate(
        [
            jnp.concatenate([right[0:1], here[1:2]], axis=1),
            jnp.concatenate([here[2:6], right[2:6]], axis=1),
            jnp.full((3, lanes), -1, jnp.int32),
        ],
        axis=0,
    )
    rate = jnp.tile(rate_block, 2)[None, :]
    vmem, smem = pl.BlockSpec(memory_space=pltpu.VMEM), pl.BlockSpec(memory_space=pltpu.SMEM)
    whole = (variables, 256, lanes)
    faces = (STEPS, 3, 64 * variables, lanes)
    pairs = pltpu.SemaphoreType.DMA((STEPS, 3))
    return pl.pallas_call(
        halo_kernel,
        out_shape=(
            jax.ShapeDtypeStruct(state_in.shape, jnp.float32),
            jax.ShapeDtypeStruct((blocks, 128), jnp.float32),
        ),
        in_specs=[vmem, smem, smem, smem, vmem, vmem],
        out_specs=(vmem, vmem),
        scratch_shapes=[
            pltpu.VMEM(whole, jnp.float32),
            pltpu.VMEM(whole, jnp.float32),
            pltpu.VMEM(whole, jnp.float32),
            pltpu.VMEM(whole, jnp.float32),
            pltpu.VMEM(faces, jnp.float32),
            pltpu.VMEM(faces, jnp.float32),
            pltpu.VMEM(faces, jnp.float32),
            pltpu.VMEM((5, 3 * lanes, lanes), jnp.bfloat16),
            pairs,
            pairs,
            pairs,
            pairs,
        ],
        compiler_params=pltpu.CompilerParams(
            collective_id=0, has_side_effects=True, vmem_limit_bytes=48 * 1024 * 1024
        ),
    )(
        state_in,
        0.5 * flux_derivative_matrices.reshape(-1),
        0.5 * speeds,
        parallel_flow_coefficients,
        rate,
        target,
    )


def fourier_tables(orders):
    longitudes = jnp.arange(NLON, dtype=jnp.int32)
    phase_index = longitudes[:, None] * orders[None, :] % NLON
    angle_rad = phase_index.astype(jnp.float32) * (2.0 * math.pi / NLON)
    return (jnp.cos(angle_rad), jnp.sin(angle_rad))


def legendre_start(sine_lat, orders):
    series_k = jnp.arange(1, DEGREES, dtype=jnp.int32).astype(jnp.float32)
    log_sums = jnp.concatenate(
        [
            jnp.zeros((1,), jnp.float32),
            jnp.cumsum(0.5 * jnp.log((2.0 * series_k + 1.0) / (2.0 * series_k))),
        ]
    )
    log_base = jnp.take(log_sums, orders)
    order_real = orders.astype(jnp.float32)
    return jnp.exp(
        0.5 * math.log(0.5) + log_base[None, :] + order_real[None, :] * jnp.log(sine_lat)[:, None]
    )


def pair_kernel(share_rows, start_ref, order_ref, cosine_ref, weight_ref, out_ref, table):
    diagonal = start_ref[...]
    height, pieces = diagonal.shape[0], diagonal.shape[1] // 128
    order = order_ref[...]
    square = order * order
    cosine = cosine_ref[...]

    def one_degree(degree, carried):
        previous, before = carried
        real = degree.astype(jnp.float32)
        top = jnp.full(diagonal.shape, 4.0 * real * real - 1.0, jnp.float32)
        lower = real - 1.0
        low = jnp.full(diagonal.shape, 4.0 * lower * lower - 1.0, jnp.float32)
        up = jnp.sqrt(jnp.maximum(top, 1.0) / jnp.maximum(real * real - square, 1.0))
        back = jnp.sqrt(jnp.maximum(lower * lower - square, 0.0) / jnp.maximum(low, 1.0))
        present = (up * cosine) * previous + (-up * back) * before
        present = present + jnp.where(order == real, diagonal, 0.0)
        at = pl.multiple_of(degree * height, height)
        for piece in range(pieces):
            table[piece, pl.ds(at, height), :] = present[:, 128 * piece : 128 * (piece + 1)]
        return present, previous

    zero = diagonal * 0.0
    lax.fori_loop(0, DEGREES, one_degree, (zero, zero), unroll=8)
    degrees = lax.broadcasted_iota(jnp.int32, (DEGREES, 1), 0).astype(jnp.float32)
    gain = POT_GAIN / (degrees * (degrees + 1.0) + KAPPA2)
    for row in range(share_rows):
        rows = jnp.concatenate(
            [table[piece, pl.ds(row, DEGREES, stride=height), :] for piece in range(pieces)], axis=1
        )
        out_ref[row] = lax.dot_general(
            rows * weight_ref[...],
            rows * gain,
            (((0,), (0,)), ((), ())),
            precision=HIGHEST_PRECISION,
            preferred_element_type=jnp.float32,
        )


def order_pairs(sine_lat, cosine_lat, weights_lat, orders):
    lat_total, share = sine_lat.shape[0], orders.shape[0]
    side = max(1, min(share, 128 // lat_total))
    share_rows, lanes = share // side, side * lat_total
    start = legendre_start(sine_lat, orders).T.reshape(side, share_rows, lat_total)
    start = jnp.swapaxes(start, 0, 1).reshape(share_rows, lanes)
    order_real = jnp.broadcast_to(
        orders.astype(jnp.float32).reshape(side, share_rows, 1), (side, share_rows, lat_total)
    )
    order_real = jnp.swapaxes(order_real, 0, 1).reshape(share_rows, lanes)
    height = -(-share_rows // 8) * 8
    start = jnp.pad(start, ((0, height - share_rows), (0, 0)))
    order_real = jnp.pad(order_real, ((0, height - share_rows), (0, 0)))
    cosine = jnp.tile(cosine_lat, side)[None, :]
    weight = jnp.tile(weights_lat, side)[None, :]
    pairs = pl.pallas_call(
        functools.partial(pair_kernel, share_rows),
        out_shape=jax.ShapeDtypeStruct((share_rows, lanes, lanes), jnp.float32),
        scratch_shapes=[pltpu.VMEM((lanes // 128, DEGREES * height, 128), jnp.float32)],
        compiler_params=pltpu.CompilerParams(vmem_limit_bytes=48 * 1024 * 1024),
    )(start, order_real, cosine, weight)
    blocks = [
        pairs[:, lat_total * at : lat_total * (at + 1), lat_total * at : lat_total * (at + 1)]
        for at in range(side)
    ]
    return jnp.concatenate(blocks, axis=0)


def solve_spectral(coef_re, coef_im, cosine_lat, sine_lat, weights_lat, orders):
    pairs = order_pairs(sine_lat, cosine_lat, weights_lat, orders)
    both = jnp.stack([coef_re.T, coef_im.T], axis=1)
    synth = jnp.einsum("rcj,rjk->crk", both, pairs, precision=HIGHEST_PRECISION)
    return (synth[0].T, synth[1].T)


def body(
    invariant_fluid_quantities,
    flux_derivative_matrices,
    levels,
    neighbours,
    block_latitude_band,
    block_longitude_segment,
    parallel_flow_coefficients,
):
    grp_size = lax.axis_size("grp")
    core_size = lax.axis_size("cores")
    device_total = grp_size * core_size
    block_portion = invariant_fluid_quantities.shape[1]
    state_variables = invariant_fluid_quantities.shape[0]
    device = lax.axis_index(("grp", "cores"))
    speeds = wave_speeds(flux_derivative_matrices)
    rate_block = COURANT * jnp.exp2(levels.astype(jnp.float32) - (LEVELS - 1)) / jnp.max(speeds)
    offset = (device - 1) * block_portion
    local_index = jnp.where(neighbours >= 0, neighbours - offset, -1)
    parallel_flow_charge, patches = advance(
        invariant_fluid_quantities,
        flux_derivative_matrices,
        speeds,
        rate_block,
        local_index,
        parallel_flow_coefficients,
    )
    band_index = block_latitude_band[:, 0]
    block_ids = jnp.arange(block_portion, dtype=jnp.int32)
    earlier = (band_index[None, :] == band_index[:, None]) & (
        block_ids[None, :] < block_ids[:, None]
    )
    rank_in_band = jnp.sum(earlier.astype(jnp.int32), axis=1)
    capacity = -(-max(2, 2 * block_portion // grp_size) // 8) * 8
    slot_index = band_index * capacity + rank_in_band
    slot_ids = jnp.arange(grp_size * capacity, dtype=jnp.int32)
    placing = (slot_ids[:, None] == slot_index[None, :]).astype(jnp.float32)
    send_rows = jnp.dot(placing, patches, precision=HIGHEST_PRECISION).reshape(
        grp_size, capacity, 128
    )
    send_codes = jnp.dot(
        placing, (block_longitude_segment + 1).astype(jnp.float32), precision=HIGHEST_PRECISION
    ).reshape(grp_size, capacity)
    message = jnp.concatenate(
        [send_rows, jnp.broadcast_to(send_codes[:, :, None], send_rows.shape)], axis=1
    )
    lat_total = LAT_DEV * device_total
    degree_share = DEGREES // device_total
    lat_ids = jnp.arange(lat_total, dtype=jnp.int32).reshape(device_total, LAT_DEV).T.reshape(-1)
    colatitude = (lat_ids.astype(jnp.float32) + 0.5) * (math.pi / lat_total)
    cosine_all = jnp.cos(colatitude)
    sine_all = jnp.sin(colatitude)
    weights_all = math.pi / lat_total * sine_all
    own_orders = device * degree_share + jnp.arange(degree_share, dtype=jnp.int32)
    pairs = order_pairs(sine_all, cosine_all, weights_all, own_orders)
    grid_rows, potential_rows, home_rows = harmonic_solve(message, pairs, device_total)

    def by_latitude(found):
        return jnp.swapaxes(found.reshape(16, LAT_DEV, 64), 0, 1).reshape(LAT_DEV, NLON)

    fac_local, potential_local = by_latitude(grid_rows), by_latitude(potential_rows)
    shell_potential = jnp.dot(placing.T, home_rows.reshape(-1, 128), precision=HIGHEST_PRECISION)
    return (parallel_flow_charge, fac_local, potential_local, shell_potential)


def solution(mesh):
    placed = (
        P(None, ("grp", "cores"), None),
        P(),
        P(("grp", "cores")),
        P(("grp", "cores"), None),
        P(("grp", "cores"), None),
        P(("grp", "cores")),
        P(),
    )
    return jax.shard_map(
        body,
        mesh=mesh,
        in_specs=placed,
        out_specs=(
            P(None, ("grp", "cores"), None),
            P(("grp", "cores"), None),
            P(("grp", "cores"), None),
            P(("grp", "cores"), None),
        ),
        check_vma=False,
    )
```

```python
import functools
import math

import jax
import jax.numpy as jnp
import numpy as np
from jax import lax
from jax.experimental import pallas as pl
from jax.experimental.pallas import tpu as pltpu
from jax.sharding import PartitionSpec as P

LEVELS = 4
STEPS = 2
LAT_DEV = 2
NLON = 1024
DEGREES = 512


COURANT = 0.3
KAPPA2 = 400.0
POT_GAIN = 2000.0
HIGHEST_PRECISION = lax.Precision.HIGHEST


def wave_speeds(flux_derivative_matrices):
    return jnp.max(jnp.sum(jnp.abs(flux_derivative_matrices), axis=2), axis=1)


def split_dot(values, picks):
    high = values.astype(jnp.bfloat16)
    low = (values - high.astype(jnp.float32)).astype(jnp.bfloat16)
    return jnp.dot(high, picks, preferred_element_type=jnp.float32) + jnp.dot(
        low, picks, preferred_element_type=jnp.float32
    )


def halo_kernel(
    state_ref, flux_ref, speed_ref, coef_ref, rate_ref, target_ref,
    start_ref, order_ref, cosine_ref, weight_ref,
    state_out, patch_out, pairs_out,
    table, cells, diffs, laps, change, own, before, after, picks,
    send_prev, send_next, recv_prev, recv_next,
):
    variables, blocks = state_ref.shape[0], state_ref.shape[1]
    lanes = 2 * blocks
    core_size = lax.axis_size("cores")
    total = lax.axis_size("grp") * core_size
    device = lax.axis_index("grp") * core_size + lax.axis_index("cores")
    has_prev, has_next = device > 0, device < total - 1
    prev_id = (lax.div(device - 1, core_size), lax.rem(device - 1 + core_size, core_size))
    next_id = (lax.div(device + 1, core_size), lax.rem(device + 1, core_size))
    mesh_type = pl.DeviceIdType.MESH
    barrier = pltpu.get_barrier_semaphore()

    @pl.when(has_prev)
    def _():
        pl.semaphore_signal(barrier, inc=1, device_id=prev_id, device_id_type=mesh_type)

    @pl.when(has_next)
    def _():
        pl.semaphore_signal(barrier, inc=1, device_id=next_id, device_id_type=mesh_type)

    @pl.when(jnp.logical_not(has_prev))
    def _():
        before[...] = jnp.zeros_like(before)

    @pl.when(jnp.logical_not(has_next))
    def _():
        after[...] = jnp.zeros_like(after)

    left_half = lax.broadcasted_iota(jnp.int32, (1, lanes), 1) < blocks
    for v in range(variables):
        both = jnp.concatenate([state_ref[v, :, 0:256], state_ref[v, :, 256:512]], axis=0)
        cells[v] = both.T

    def copies(step, direction):
        to_prev = pltpu.make_async_remote_copy(
            src_ref=own.at[step, direction], dst_ref=after.at[step, direction],
            send_sem=send_prev.at[step, direction], recv_sem=recv_next.at[step, direction],
            device_id=prev_id, device_id_type=mesh_type,
        )
        to_next = pltpu.make_async_remote_copy(
            src_ref=own.at[step, direction], dst_ref=before.at[step, direction],
            send_sem=send_next.at[step, direction], recv_sem=recv_prev.at[step, direction],
            device_id=next_id, device_id_type=mesh_type,
        )
        return to_prev, to_next

    def start(step, direction):
        to_prev, to_next = copies(step, direction)

        @pl.when(has_prev)
        def _():
            to_prev.start()

        @pl.when(has_next)
        def _():
            to_next.start()

    def arrive(step, direction):
        to_prev, to_next = copies(step, direction)

        @pl.when(has_prev)
        def _():
            to_next.wait_recv()

        @pl.when(has_next)
        def _():
            to_prev.wait_recv()

    def left(step, direction):
        to_prev, to_next = copies(step, direction)

        @pl.when(has_prev)
        def _():
            to_prev.wait_send()

        @pl.when(has_next)
        def _():
            to_next.wait_send()

    def fill(step, direction):
        for v in range(variables):
            if direction == 0:
                own[step, 0, pl.ds(64 * v, 64), :] = jnp.where(
                    left_half, cells[v, 0:64, :], cells[v, 192:256, :]
                )
            elif direction == 1:
                for side in range(2):
                    for x in range(4):
                        own[step, 1, pl.ds(256 * side + 32 * v + 8 * x, 8), :] = cells[
                            v, pl.ds(64 * x + 56 * side, 8), :
                        ]
            else:
                for side in range(2):
                    own[step, 2, pl.ds(256 * side + 32 * v, 32), :] = cells[
                        v, pl.ds(7 * side, 32, stride=8), :
                    ]

    def gathered(step, direction, first, rows, face):
        part = pl.ds(first, rows)
        table = jnp.concatenate(
            [before[step, direction, part, :], own[step, direction, part, :], after[step, direction, part, :]],
            axis=1,
        )
        return split_dot(table, picks[face])

    def keep(v, at, rows, lower, upper, here):
        diffs[v, pl.ds(at, rows), :] = upper - lower
        laps[v, pl.ds(at, rows), :] = upper - 2.0 * here + lower

    def sides(step, direction):
        if direction == 0:
            known = target_ref[0:1, :] >= 0
            ghosts = gathered(step, 0, 0, 64 * variables, 0)
            for v in range(variables):
                ghost = jnp.where(known, ghosts[64 * v : 64 * v + 64], own[step, 0, pl.ds(64 * v, 64), :])
                slabs = [cells[v, pl.ds(64 * x, 64), :] for x in range(4)]
                first = jnp.where(left_half, ghost, pltpu.roll(slabs[3], blocks, 1))
                last = jnp.where(left_half, pltpu.roll(slabs[0], blocks, 1), ghost)
                line = [first] + slabs + [last]
                for x in range(4):
                    keep(v, 64 * x, 64, line[x], line[x + 2], slabs[x])
            return
        near, far = 2 * direction - 1, 2 * direction
        rows = 32 * variables
        low = gathered(step, direction, rows, rows, near)
        high = gathered(step, direction, 0, rows, far)
        know_low, know_high = target_ref[near : near + 1, :] >= 0, target_ref[far : far + 1, :] >= 0
        for v in range(variables):
            part = slice(32 * v, 32 * v + 32)
            low_v = jnp.where(know_low, low[part], own[step, direction, pl.ds(32 * v, 32), :])
            high_v = jnp.where(know_high, high[part], own[step, direction, pl.ds(rows + 32 * v, 32), :])
            if direction == 1:
                for x in range(4):
                    slab = cells[v, pl.ds(64 * x, 64), :]
                    lower = jnp.concatenate([low_v[8 * x : 8 * x + 8], slab[0:56]], axis=0)
                    upper = jnp.concatenate([slab[8:64], high_v[8 * x : 8 * x + 8]], axis=0)
                    keep(v, 64 * x, 64, lower, upper, slab)
            else:
                whole = cells[v].reshape(32, 8, lanes)
                height = lax.broadcasted_iota(jnp.int32, (32, 8, lanes), 1)
                lower = jnp.where(height == 0, low_v[:, None, :], pltpu.roll(whole, 1, 1))
                upper = jnp.where(height == 7, high_v[:, None, :], pltpu.roll(whole, 7, 1))
                keep(v, 0, 256, lower.reshape(256, lanes), upper.reshape(256, lanes), cells[v])

    def mix(direction, final):
        rows = 16

        def one_chunk(chunk, carry):
            part = pl.ds(pl.multiple_of(chunk * rows, rows), rows)
            steps = [diffs[v, part, :] for v in range(variables)]
            for i in range(variables):
                total_i = -speed_ref[direction] * laps[i, part, :]
                for j in range(variables):
                    total_i = total_i + flux_ref[(direction * variables + i) * variables + j] * steps[j]
                if direction > 0:
                    total_i = total_i + change[i, part, :]
                if final:
                    cells[i, part, :] = cells[i, part, :] - rate_ref[0:1, :] * total_i
                else:
                    change[i, part, :] = total_i
            return carry

        lax.fori_loop(0, 256 // rows, one_chunk, 0)

    fill(0, 0)

    pl.semaphore_wait(barrier, has_prev.astype(jnp.int32) + has_next.astype(jnp.int32))
    for step in range(STEPS):
        for direction in range(3):
            if step > 0 or direction > 0:
                fill(step, direction)
            start(step, direction)
        if step == 0:
            row_ids = lax.broadcasted_iota(jnp.int32, (3 * lanes, lanes), 0)
            for face in range(5):
                hit = row_ids == target_ref[face : face + 1, :]
                picks[face] = hit.astype(jnp.float32).astype(jnp.bfloat16)
            pair_kernel(
                pairs_out.shape[0], start_ref, order_ref, cosine_ref, weight_ref, pairs_out, table
            )
        for direction in range(3):
            arrive(step, direction)
            sides(step, direction)
            mix(direction, direction == 2)
    for v in range(variables):
        flat = cells[v].T
        state_out[v, :, 0:256] = flat[0:blocks]
        state_out[v, :, 256:512] = flat[blocks:lanes]
    layers = []
    for z in range(2):
        layer = coef_ref[0] * cells[0, pl.ds(z, 32, stride=8), :]
        for v in range(1, variables):
            layer = layer + coef_ref[v] * cells[v, pl.ds(z, 32, stride=8), :]
        layers.append(layer)
    turned = jnp.concatenate(layers + layers, axis=0).T
    for z in range(2):
        for half in range(2):
            patch_out[:, pl.ds(64 * z + 32 * half, 32)] = turned[
                blocks * half : blocks * half + blocks, 32 * z : 32 * z + 32
            ]
    for step in range(STEPS):
        for direction in range(3):
            left(step, direction)


def advance(state_in, flux_derivative_matrices, speeds, rate_block, local_index, parallel_flow_coefficients, terms, share_rows):
    variables, blocks = state_in.shape[0], state_in.shape[1]
    lanes = 2 * blocks
    here = jnp.where(
        local_index >= 0, local_index // blocks * lanes + local_index % blocks, -1
    ).T
    right = jnp.where(here >= 0, here + blocks, -1)
    target = jnp.concatenate(
        [
            jnp.concatenate([right[0:1], here[1:2]], axis=1),
            jnp.concatenate([here[2:6], right[2:6]], axis=1),
            jnp.full((3, lanes), -1, jnp.int32),
        ],
        axis=0,
    )
    rate = jnp.tile(rate_block, 2)[None, :]
    vmem, smem = pl.BlockSpec(memory_space=pltpu.VMEM), pl.BlockSpec(memory_space=pltpu.SMEM)
    width = terms[0].shape[1]
    whole = (variables, 256, lanes)
    faces = (STEPS, 3, 64 * variables, lanes)
    pairs = pltpu.SemaphoreType.DMA((STEPS, 3))
    return pl.pallas_call(
        halo_kernel,
        out_shape=(
            jax.ShapeDtypeStruct(state_in.shape, jnp.float32),
            jax.ShapeDtypeStruct((blocks, 128), jnp.float32),
            jax.ShapeDtypeStruct((share_rows, width, width), jnp.float32),
        ),
        in_specs=[vmem, smem, smem, smem, vmem, vmem] + [vmem] * 4,
        out_specs=(vmem, vmem, vmem),
        scratch_shapes=[
            pltpu.VMEM((width // 128, DEGREES * terms[0].shape[0], 128), jnp.float32),
            pltpu.VMEM(whole, jnp.float32),
            pltpu.VMEM(whole, jnp.float32),
            pltpu.VMEM(whole, jnp.float32),
            pltpu.VMEM(whole, jnp.float32),
            pltpu.VMEM(faces, jnp.float32),
            pltpu.VMEM(faces, jnp.float32),
            pltpu.VMEM(faces, jnp.float32),
            pltpu.VMEM((5, 3 * lanes, lanes), jnp.bfloat16),
            pairs,
            pairs,
            pairs,
            pairs,
        ],
        compiler_params=pltpu.CompilerParams(
            collective_id=0, has_side_effects=True, vmem_limit_bytes=48 * 1024 * 1024
        ),
    )(
        state_in,
        0.5 * flux_derivative_matrices.reshape(-1),
        0.5 * speeds,
        parallel_flow_coefficients,
        rate,
        target,
        *terms,
    )


def legendre_start(sine_lat, orders):
    series_k = jnp.arange(1, DEGREES, dtype=jnp.int32).astype(jnp.float32)
    log_sums = jnp.concatenate(
        [
            jnp.zeros((1,), jnp.float32),
            jnp.cumsum(0.5 * jnp.log((2.0 * series_k + 1.0) / (2.0 * series_k))),
        ]
    )
    log_base = jnp.take(log_sums, orders)
    order_real = orders.astype(jnp.float32)
    return jnp.exp(
        0.5 * math.log(0.5) + log_base[None, :] + order_real[None, :] * jnp.log(sine_lat)[:, None]
    )


def pair_kernel(share_rows, start_ref, order_ref, cosine_ref, weight_ref, out_ref, table):
    diagonal = start_ref[...]
    height, pieces = diagonal.shape[0], diagonal.shape[1] // 128
    order = order_ref[...]
    square = order * order
    cosine = cosine_ref[...]

    def one_degree(degree, carried):
        previous, before = carried
        real = degree.astype(jnp.float32)
        top = jnp.full(diagonal.shape, 4.0 * real * real - 1.0, jnp.float32)
        lower = real - 1.0
        low = jnp.full(diagonal.shape, 4.0 * lower * lower - 1.0, jnp.float32)
        up = jnp.sqrt(jnp.maximum(top, 1.0) / jnp.maximum(real * real - square, 1.0))
        back = jnp.sqrt(jnp.maximum(lower * lower - square, 0.0) / jnp.maximum(low, 1.0))
        present = (up * cosine) * previous + (-up * back) * before
        present = present + jnp.where(order == real, diagonal, 0.0)
        at = pl.multiple_of(degree * height, height)
        for piece in range(pieces):
            table[piece, pl.ds(at, height), :] = present[:, 128 * piece : 128 * (piece + 1)]
        return present, previous

    zero = diagonal * 0.0
    lax.fori_loop(0, DEGREES, one_degree, (zero, zero), unroll=8)
    degrees = lax.broadcasted_iota(jnp.int32, (DEGREES, 1), 0).astype(jnp.float32)
    gain = POT_GAIN / (degrees * (degrees + 1.0) + KAPPA2)
    for row in range(share_rows):
        rows = jnp.concatenate(
            [table[piece, pl.ds(row, DEGREES, stride=height), :] for piece in range(pieces)], axis=1
        )
        out_ref[row] = lax.dot_general(
            rows * weight_ref[...],
            rows * gain,
            (((0,), (0,)), ((), ())),
            precision=HIGHEST_PRECISION,
            preferred_element_type=jnp.float32,
        )


def order_terms(sine_lat, cosine_lat, weights_lat, orders):
    lat_total, share = sine_lat.shape[0], orders.shape[0]
    side = max(1, min(share, 128 // lat_total))
    share_rows, lanes = share // side, side * lat_total
    start = legendre_start(sine_lat, orders).T.reshape(side, share_rows, lat_total)
    start = jnp.swapaxes(start, 0, 1).reshape(share_rows, lanes)
    order_real = jnp.broadcast_to(
        orders.astype(jnp.float32).reshape(side, share_rows, 1), (side, share_rows, lat_total)
    )
    order_real = jnp.swapaxes(order_real, 0, 1).reshape(share_rows, lanes)
    height = -(-share_rows // 8) * 8
    start = jnp.pad(start, ((0, height - share_rows), (0, 0)))
    order_real = jnp.pad(order_real, ((0, height - share_rows), (0, 0)))
    cosine = jnp.tile(cosine_lat, side)[None, :]
    weight = jnp.tile(weights_lat, side)[None, :]
    return start, order_real, cosine, weight


def order_blocks(pairs, lat_total, share):
    side = share // pairs.shape[0]
    blocks = [
        pairs[:, lat_total * at : lat_total * (at + 1), lat_total * at : lat_total * (at + 1)]
        for at in range(side)
    ]
    return jnp.concatenate(blocks, axis=0)


def exact_dot(left, right, contract):
    return lax.dot_general(
        left, right, (contract, ((), ())),
        precision=HIGHEST_PRECISION, preferred_element_type=jnp.float32,
    )


def wave_constants():
    order = np.arange(128) // 8
    used = (np.arange(128) % 8 < 2)[:, None]
    seg = 2.0 * np.pi / 16 * order[:, None] * np.arange(16)[None, :]
    turn = 2.0 * np.pi / NLON * order[:, None] * (np.arange(128) % 64)[None, :]
    high = 2.0 * np.pi / 64 * np.arange(DEGREES // 16)[:, None] * np.arange(64)[None, :]
    factor = np.full((DEGREES // 16, 128), 2.0)
    factor[0, :8] = 1.0
    listed = [np.cos(seg) * used, np.sin(seg) * used, np.cos(turn), np.sin(turn)]
    listed += [np.cos(high), np.sin(high), factor]
    return [jnp.asarray(one, jnp.float32) for one in listed]


def harmonic_kernel(
    share, message_ref, pairs_ref, seg_cos, seg_sin, turn_cos, turn_sin, high_cos, high_sin, factor_ref,
    grid_out, potential_out, home_out,
    got, coef_send, coef_got, waves, solved, synth_send, synth_got, back_send, home,
    send_a, recv_a, send_b, recv_b, send_c, recv_c, send_d, recv_d,
):
    core_size, groups = lax.axis_size("cores"), lax.axis_size("grp")
    total = core_size * groups
    group, core = lax.axis_index("grp"), lax.axis_index("cores")
    device = group * core_size + core
    mesh_type = pl.DeviceIdType.MESH
    barrier = pltpu.get_barrier_semaphore()

    def greet(k, carry):
        peer = lax.rem(device + k, total)
        pl.semaphore_signal(
            barrier, inc=1,
            device_id=(lax.div(peer, core_size), lax.rem(peer, core_size)), device_id_type=mesh_type,
        )
        return carry

    lax.fori_loop(1, total, greet, 0)

    def exchange(source, target, send, recv, over_all, pick):
        count, me = (total, device) if over_all else (groups, group)

        def copy(k):
            peer = lax.rem(me + k, count)
            where = (lax.div(peer, core_size), lax.rem(peer, core_size)) if over_all else (peer, core)
            return pltpu.make_async_remote_copy(
                src_ref=source.at[pick(peer)], dst_ref=target.at[me],
                send_sem=send.at[k], recv_sem=recv.at[k],
                device_id=where, device_id_type=mesh_type,
            )

        def begin(k, carry):
            copy(k).start()
            return carry

        def finish(k, carry):
            copy(k).wait_recv()
            return carry

        def drain(k, carry):
            copy(k).wait_send()
            return carry

        lax.fori_loop(1, count, begin, 0)
        target[me] = source[pick(me)]
        return lambda: lax.fori_loop(1, count, finish, 0), lambda: lax.fori_loop(1, count, drain, 0)

    same = lambda peer: peer
    pl.semaphore_wait(barrier, total - 1)
    arrived, drain_a = exchange(message_ref, got, send_a, recv_a, False, same)
    capacity = message_ref.shape[1] // 2
    slots = groups * capacity
    arrived()
    rows = got[:, 0:capacity, :].reshape(slots, 128)
    codes = got[:, capacity : 2 * capacity, :].reshape(slots, 128)
    seg_ids = lax.broadcasted_iota(jnp.int32, (slots, 128), 1).astype(jnp.float32) + 1.0
    landing = (codes == seg_ids).astype(jnp.float32)
    grid = exact_dot(landing, rows, ((0,), (0,)))[0:16]
    grid_out[...] = grid
    near_re = exact_dot(seg_cos[...], grid, ((1,), (0,)))
    near_im = -exact_dot(seg_sin[...], grid, ((1,), (0,)))
    mid_re = near_re * turn_cos[...] + near_im * turn_sin[...]
    mid_im = near_im * turn_cos[...] - near_re * turn_sin[...]
    real_row = lax.broadcasted_iota(jnp.int32, (128, 128), 0) % 8 == 0
    with_cos = jnp.where(real_row, mid_re, mid_im)
    with_sin = jnp.where(real_row, mid_im, -mid_re)
    for z in range(2):
        lat = slice(64 * z, 64 * z + 64)
        coef = exact_dot(high_cos[...], with_cos[:, lat], ((1,), (1,)))
        coef = coef + exact_dot(high_sin[...], with_sin[:, lat], ((1,), (1,)))
        coef_send[:, z, :] = coef / NLON
    arrived, drain_b = exchange(
        coef_send, coef_got, send_b, recv_b, True, lambda peer: lax.div(peer * share, 16)
    )
    arrived()
    cut = jnp.concatenate([coef_got[:, z, :].T for z in range(2)], axis=1)
    waves[...] = cut.reshape(16, 8, 2 * total)
    if share < 16:
        solved[...] = jnp.zeros_like(solved)
    first = lax.rem(share * device, 16)
    for order in range(share):
        solved[first + order] = exact_dot(waves[first + order], pairs_ref[order], ((1,), (0,)))
    back = solved[...].reshape(128, 2 * total).T
    for z in range(2):
        synth_send[:, z, :] = back[z * total : (z + 1) * total]
    arrived, drain_c = exchange(synth_send, synth_got, send_c, recv_c, True, same)
    arrived()
    parts_cos, parts_sin = [], []
    for z in range(2):
        part = synth_got[:, z, :]
        if total > DEGREES // 16:
            part = jnp.sum(part.reshape(DEGREES // 16, total * 16 // DEGREES, 128), axis=1)
        part = part * factor_ref[...]
        parts_cos.append(exact_dot(part, high_cos[...], ((0,), (0,))))
        parts_sin.append(exact_dot(part, high_sin[...], ((0,), (0,))))
    full_cos, full_sin = jnp.concatenate(parts_cos, axis=1), jnp.concatenate(parts_sin, axis=1)
    alpha = full_cos * turn_cos[...] - full_sin * turn_sin[...]
    beta = full_cos * turn_sin[...] + full_sin * turn_cos[...]
    potential = exact_dot(seg_cos[...], jnp.where(real_row, alpha, -beta), ((0,), (0,)))
    potential = potential - exact_dot(seg_sin[...], jnp.where(real_row, beta, alpha), ((0,), (0,)))
    potential_out[...] = potential
    spread = exact_dot(landing[:, 0:16], potential, ((1,), (0,)))
    back_send[...] = spread.reshape(groups, capacity, 128)
    arrived, drain_d = exchange(back_send, home, send_d, recv_d, False, same)
    arrived()
    home_out[...] = home[...]
    drain_a()
    drain_b()
    drain_c()
    drain_d()


def harmonic_solve(message, pairs, total):
    groups, capacity = message.shape[0], message.shape[1] // 2
    share = pairs.shape[0]
    wide = DEGREES // 16
    vmem = pl.BlockSpec(memory_space=pltpu.VMEM)
    few, many = pltpu.SemaphoreType.DMA((groups,)), pltpu.SemaphoreType.DMA((total,))
    room = lambda *shape: pltpu.VMEM(shape, jnp.float32)
    result = lambda *shape: jax.ShapeDtypeStruct(shape, jnp.float32)
    return pl.pallas_call(
        functools.partial(harmonic_kernel, share),
        out_shape=(result(16, 128), result(16, 128), result(groups, capacity, 128)),
        in_specs=[vmem] * 9,
        out_specs=(vmem, vmem, vmem),
        scratch_shapes=[
            room(groups, 2 * capacity, 128),
            room(wide, 2, 128),
            room(total, 2, 128),
            room(16, 8, 2 * total),
            room(16, 8, 2 * total),
            room(total, 2, 128),
            room(total, 2, 128),
            room(groups, capacity, 128),
            room(groups, capacity, 128),
            few, few, many, many, many, many, few, few,
        ],
        compiler_params=pltpu.CompilerParams(
            collective_id=1, has_side_effects=True, vmem_limit_bytes=48 * 1024 * 1024
        ),
    )(message, pairs, *wave_constants())


def body(
    invariant_fluid_quantities,
    flux_derivative_matrices,
    levels,
    neighbours,
    block_latitude_band,
    block_longitude_segment,
    parallel_flow_coefficients,
):
    grp_size = lax.axis_size("grp")
    core_size = lax.axis_size("cores")
    device_total = grp_size * core_size
    block_portion = invariant_fluid_quantities.shape[1]
    state_variables = invariant_fluid_quantities.shape[0]
    device = lax.axis_index(("grp", "cores"))
    speeds = wave_speeds(flux_derivative_matrices)
    rate_block = COURANT * jnp.exp2(levels.astype(jnp.float32) - (LEVELS - 1)) / jnp.max(speeds)
    offset = (device - 1) * block_portion
    local_index = jnp.where(neighbours >= 0, neighbours - offset, -1)
    lat_total = LAT_DEV * device_total
    degree_share = DEGREES // device_total
    lat_ids = jnp.arange(lat_total, dtype=jnp.int32).reshape(device_total, LAT_DEV).T.reshape(-1)
    colatitude = (lat_ids.astype(jnp.float32) + 0.5) * (math.pi / lat_total)
    cosine_all = jnp.cos(colatitude)
    sine_all = jnp.sin(colatitude)
    weights_all = math.pi / lat_total * sine_all
    own_orders = device * degree_share + jnp.arange(degree_share, dtype=jnp.int32)
    terms = order_terms(sine_all, cosine_all, weights_all, own_orders)
    share_rows = degree_share * lat_total // terms[0].shape[1]
    parallel_flow_charge, patches, pairs = advance(
        invariant_fluid_quantities,
        flux_derivative_matrices,
        speeds,
        rate_block,
        local_index,
        parallel_flow_coefficients,
        terms,
        share_rows,
    )
    band_index = block_latitude_band[:, 0]
    block_ids = jnp.arange(block_portion, dtype=jnp.int32)
    earlier = (band_index[None, :] == band_index[:, None]) & (
        block_ids[None, :] < block_ids[:, None]
    )
    rank_in_band = jnp.sum(earlier.astype(jnp.int32), axis=1)
    capacity = -(-max(2, 2 * block_portion // grp_size) // 8) * 8
    slot_index = band_index * capacity + rank_in_band
    slot_ids = jnp.arange(grp_size * capacity, dtype=jnp.int32)
    placing = (slot_ids[:, None] == slot_index[None, :]).astype(jnp.float32)
    send_rows = jnp.dot(placing, patches, precision=HIGHEST_PRECISION).reshape(
        grp_size, capacity, 128
    )
    send_codes = jnp.dot(
        placing, (block_longitude_segment + 1).astype(jnp.float32), precision=HIGHEST_PRECISION
    ).reshape(grp_size, capacity)
    message = jnp.concatenate(
        [send_rows, jnp.broadcast_to(send_codes[:, :, None], send_rows.shape)], axis=1
    )
    pairs = order_blocks(pairs, lat_total, degree_share)
    grid_rows, potential_rows, home_rows = harmonic_solve(message, pairs, device_total)

    def by_latitude(found):
        return jnp.swapaxes(found.reshape(16, LAT_DEV, 64), 0, 1).reshape(LAT_DEV, NLON)

    fac_local, potential_local = by_latitude(grid_rows), by_latitude(potential_rows)
    shell_potential = jnp.dot(placing.T, home_rows.reshape(-1, 128), precision=HIGHEST_PRECISION)
    return (parallel_flow_charge, fac_local, potential_local, shell_potential)


def solution(mesh):
    placed = (
        P(None, ("grp", "cores"), None),
        P(),
        P(("grp", "cores")),
        P(("grp", "cores"), None),
        P(("grp", "cores"), None),
        P(("grp", "cores")),
        P(),
    )
    return jax.shard_map(
        body,
        mesh=mesh,
        in_specs=placed,
        out_specs=(
            P(None, ("grp", "cores"), None),
            P(("grp", "cores"), None),
            P(("grp", "cores"), None),
            P(("grp", "cores"), None),
        ),
        check_vma=False,
    )
```
